256 devices in a mesh: rx: 4 (over z_hi, core), ry: 4 (over x), fsdp: 16 (over y, z_lo).
Axes of the slice: x: 4, y: 4, z: 8 (z_hi: 2, z_lo: 4; z = z_hi * 4 + z_lo), core: 2. Of those that a mesh axis runs over, the one named last changes fastest.
Arguments:
- inputs: bfloat16 [4, 4, 2, 2048, 4096], P('rx', 'ry', None, 'fsdp'), may hold values from -6 to 6
- value_grad: bfloat16 [4, 4, 2, 2048, 1024], P('rx', 'ry', None, 'fsdp'), may hold values from -0.099609375 to 0.099609375
- weight: float32 [4, 4, 4096, 1024], P('rx', 'ry', 'fsdp'), may hold values from -6 to 6
- weight_m: float32 [4, 4, 4096, 1024], P('rx', 'ry', 'fsdp'), may hold values from -3 to 3
- weight_v: float32 [4, 4, 4096, 1024], P('rx', 'ry', 'fsdp'), may hold values from 0.001 to 0.1
- gain: float32 [4, 4, 4096], P('rx', 'ry', 'fsdp'), may hold values from 0.5 to 1.5
- gain_m: float32 [4, 4, 4096], P('rx', 'ry', 'fsdp'), may hold values from -3 to 3
- gain_v: float32 [4, 4, 4096], P('rx', 'ry', 'fsdp'), may hold values from 0.001 to 0.1
- mixing: int32 [4, 4, 5], P('rx', 'ry'), may hold values from 1 to 8
Outputs:
- input_grad: float32 [4, 4, 2, 2048, 4096], P('rx', 'ry', None, 'fsdp')
- new_weight: float32 [4, 4, 4096, 1024], P('rx', 'ry', 'fsdp')
- new_weight_m: float32 [4, 4, 4096, 1024], P('rx', 'ry', 'fsdp')
- new_weight_v: float32 [4, 4, 4096, 1024], P('rx', 'ry', 'fsdp')
- new_gain: float32 [4, 4, 4096], P('rx', 'ry', 'fsdp')
- new_gain_m: float32 [4, 4, 4096], P('rx', 'ry', 'fsdp')
- new_gain_v: float32 [4, 4, 4096], P('rx', 'ry', 'fsdp')
The draws below stay inside these ranges and needn't reach their ends.
All inputs are finite; a program needn't handle non-finite values.
Results may differ from the reference program's by a relative error of at most 0.0042.
Values may be sent and summed in bfloat16 or wider, within the bound.
A program may use at most 128 MiB of HBM per device.

```python
import math
import jax
import jax.numpy as jnp
from jax import lax

D = 4096
KV = 1024
MB = 2
TOKENS = 2048
RX = 4
RY = 4


def plant(values, rng, low, top_value):
    extent = values.shape
    index_at = [jax.random.randint(jax.random.fold_in(rng, axis), (), 0, extent[axis]) for axis in range(len(extent))]
    values = values.at[tuple(index_at)].set(low)
    longest = extent.index(max(extent))
    index_at[longest] = (index_at[longest] + 1) % extent[longest]
    return values.at[tuple(index_at)].set(top_value)


def shard_levels(stream_key, extent, shards, smallest, largest):
    factor_of = 1.0
    for axis_at, parts in shards:
        steps = jax.random.uniform(jax.random.fold_in(jax.random.fold_in(stream_key, 6), axis_at), (parts,), jnp.float32, smallest / len(shards), largest / len(shards))
        factor_of = factor_of * jnp.repeat(jnp.exp(steps), extent[axis_at] // parts).reshape((-1,) + (1,) * (len(extent) - 1 - axis_at))
    return factor_of


def normal_values(key, shape, width, limit, split=(), held_as=jnp.bfloat16):
    entries = jax.random.normal(key, shape, jnp.float32) * width
    if len(split) > 0:
        entries = shard_levels(key, shape, split, -0.22, 0.18) * entries
    return jnp.clip(entries, min=-limit, max=limit).astype(held_as)


def setup_inputs(seed: int = 0) -> dict:
    key_of = jax.random.split(jax.random.key(seed), 10)
    return {
        "inputs": normal_values(key_of[0], (RX, RY, MB, TOKENS, D), 1.0, 6.0, ((0, 4), (1, 4), (3, 16))),
        "value_grad": normal_values(key_of[1], (RX, RY, MB, TOKENS, KV), 0.015625, 0.099609375, ((0, 4), (1, 4), (3, 16))),
        "weight": normal_values(key_of[2], (RX, RY, D, KV), 1.0, 6.0, ((0, 4), (1, 4), (2, 16)), jnp.float32),
        "weight_m": normal_values(key_of[3], (RX, RY, D, KV), 0.5, 3.0, ((0, 4), (1, 4), (2, 16)), jnp.float32),
        "weight_v": jnp.clip(jnp.exp(math.log(0.1) - 4.6051702 * jax.random.uniform(key_of[4], (RX, RY, D, KV), jnp.float32) ** shard_levels(key_of[4], (RX, RY, D, KV), ((0, 4), (1, 4), (2, 16)), -0.2, 0.2)), 0.001, 0.1),
        "gain": jnp.clip(1.0 + 0.1 * jax.random.normal(key_of[5], (RX, RY, D), jnp.float32), 0.5, 1.5),
        "gain_m": normal_values(key_of[6], (RX, RY, D), 0.5, 3.0, ((0, 4), (1, 4), (2, 16)), jnp.float32),
        "gain_v": jnp.clip(jnp.exp(math.log(0.1) - 4.6051702 * jax.random.uniform(key_of[7], (RX, RY, D), jnp.float32) ** shard_levels(key_of[7], (RX, RY, D), ((0, 4), (1, 4), (2, 16)), -0.2, 0.2)), 0.001, 0.1),
        "mixing": plant(jax.random.randint(key_of[8], (RX, RY, 5), 1, 9), jax.random.fold_in(key_of[8], 1), 1, 8).astype(jnp.int32),
    }


def replica_step(packed):
    acts, cotangent, weight, weight_m, weight_v, gain, gain_m, gain_v = packed
    count_rows = acts.shape[0] * acts.shape[1]
    flat_acts = acts.reshape(count_rows, acts.shape[2]).astype(jnp.float32)
    flat_cot = cotangent.reshape(count_rows, cotangent.shape[2])
    scale = lax.rsqrt(lax.optimization_barrier(jnp.mean(flat_acts * flat_acts, axis=1, keepdims=True)) + 1e-05)
    unit = flat_acts * scale
    normalized = unit.astype(jnp.bfloat16)
    weight_low = weight.astype(jnp.bfloat16)
    gain_low = gain.astype(jnp.bfloat16).astype(jnp.float32)
    out_grad = jnp.dot(flat_cot, weight_low.T, preferred_element_type=jnp.float32)
    grad_gain = lax.optimization_barrier(jnp.sum(out_grad * unit, axis=0))
    unit_grad = out_grad * gain_low[None, :]
    inner = lax.optimization_barrier(jnp.mean(unit_grad * unit, axis=1, keepdims=True))
    input_grad = scale * (unit_grad - unit * inner)
    summed = jnp.dot(normalized.T, flat_cot, preferred_element_type=jnp.float32)
    grad_weight = gain_low[:, None] * summed
    new_wm = 0.9 * weight_m + 0.1 * grad_weight
    new_wv = 0.999 * weight_v + 0.001 * grad_weight * grad_weight
    stepped_w = weight - 0.01 * (new_wm / (jnp.sqrt(new_wv) + 1e-08) + 0.1 * weight)
    new_gm = 0.9 * gain_m + 0.1 * grad_gain
    new_gv = 0.999 * gain_v + 0.001 * grad_gain * grad_gain
    stepped_g = gain - 0.01 * new_gm / (jnp.sqrt(new_gv) + 1e-08)
    return (input_grad.reshape(acts.shape), stepped_w, new_wm, new_wv, stepped_g, new_gm, new_gv)

def mix_torus(stepped, before, share):
    extra = (1,) * (before.ndim - 2)

    def weighted(index, value):
        return share[:, :, index].reshape(share.shape[:2] + extra) * value
    total = weighted(0, stepped)
    total = total + weighted(1, jnp.roll(before, 1, 0))
    total = total + weighted(2, jnp.roll(before, -1, 0))
    total = total + weighted(3, jnp.roll(before, 1, 1))
    total = total + weighted(4, jnp.roll(before, -1, 1))
    return total

def reference(inputs, value_grad, weight, weight_m, weight_v, gain, gain_m, gain_v, mixing):

    def flatten(array):
        return array.reshape((RX * RY,) + array.shape[2:])
    packed = tuple((flatten(a) for a in (inputs, value_grad, weight, weight_m, weight_v, gain, gain_m, gain_v)))
    results = lax.map(replica_step, packed)
    input_grad, stepped_w, new_wm, new_wv, stepped_g, new_gm, new_gv = [r.reshape((RX, RY) + r.shape[1:]) for r in results]
    raw_share = mixing.astype(jnp.float32)
    share = raw_share / lax.optimization_barrier(jnp.sum(raw_share, axis=2, keepdims=True))
    new_weight = mix_torus(stepped_w, weight, share)
    new_gain = mix_torus(stepped_g, gain, share)
    return (input_grad, new_weight, new_wm, new_wv, new_gain, new_gm, new_gv)
```

```python
import jax
import jax.numpy as jnp
from jax import lax
from jax.experimental import pallas as pl
from jax.experimental.pallas import tpu as pltpu
from jax.sharding import PartitionSpec as P

MESH = pl.DeviceIdType.MESH
F32 = jnp.float32
BF16 = jnp.bfloat16

ROWS = 256
BLK = 256
KV = 1024
WIDE = 1024
WROWS = BLK + 16

VG = 0
WL = 6
WR = 10
NS = 14
US = 26
RR = 38
RL = 42
GG = 46
GO = 49
NSEM = 53


def step_kernel(
    mix, x_hbm, vg_hbm, w_hbm, m_hbm, v_hbm, gain, gain_m, gain_v,
    ig, nw, nm, nv, ng, ngm, ngv,
    xv, wf, mv, vv, vgp, nown, npool, npt, wp, us, ur, gbuf, rsend, rr, rl, gg, ggr, gos, sc, gcol,
    lsem, ssem, rsem,
):
    rx = lax.axis_index("rx")
    ry = lax.axis_index("ry")
    f = lax.axis_index("fsdp")
    zh = rx // 2
    core = rx % 2
    y = f // 4
    z = f % 4

    def dev(yy, zz):
        return (rx, ry, yy * 4 + zz)

    def ypeer(r):
        return dev((y + r) % 4, z)

    far_rx = (1 - zh) * 2 + (1 - core)
    chip_rx = zh * 2 + (1 - core)

    def remote(src, dst, k, device):
        return pltpu.make_async_remote_copy(
            src_ref=src, dst_ref=dst, send_sem=ssem.at[k], recv_sem=rsem.at[k],
            device_id=device, device_id_type=MESH,
        )

    loads = [
        pltpu.make_async_copy(w_hbm, wf, lsem.at[0]),
        pltpu.make_async_copy(x_hbm, xv, lsem.at[1]),
        pltpu.make_async_copy(vg_hbm, vgp.at[pl.ds(0, ROWS)], lsem.at[2]),
        pltpu.make_async_copy(m_hbm, mv, lsem.at[3]),
        pltpu.make_async_copy(v_hbm, vv, lsem.at[4]),
    ]
    for c in loads:
        c.start()

    barrier = pltpu.get_barrier_semaphore()
    far_base = (1 - z // 2) * 2
    partners = [ypeer(1), ypeer(2), ypeer(3)]
    partners += [dev(y, (z + 1) % 4), dev(y, (z + 2) % 4), dev(y, (z + 3) % 4)]
    partners += [(rx, (ry + 1) % 4, f), (rx, (ry + 3) % 4, f), (chip_rx, ry, f)]
    partners += [(far_rx, ry, y * 4 + far_base), (far_rx, ry, y * 4 + far_base + 1)]
    for p in partners:
        pl.semaphore_signal(barrier, inc=1, device_id=p, device_id_type=MESH)
    pl.semaphore_wait(barrier, len(partners))

    sent = []

    def go(copy, cond=None):
        copy.start()
        sent.append((cond, copy))

    def half(ref, slot, h):
        return ref.at[pl.ds(slot * ROWS + h * (ROWS // 2), ROWS // 2)]

    go(remote(half(vg_hbm, 0, 0), half(vgp, 1, 0), VG + 0, ypeer(1)))
    go(remote(half(vg_hbm, 0, 1), half(vgp, 3, 1), VG + 1, ypeer(3)))
    go(remote(half(vg_hbm, 0, 1), half(vgp, 1, 1), VG + 2, ypeer(1)))
    go(remote(half(vg_hbm, 0, 0), half(vgp, 3, 0), VG + 3, ypeer(3)))

    loads[0].wait()
    gain_row = gain[0].astype(BF16)

    def cast_rows(i, carry):
        rows = pl.ds(pl.multiple_of(i * 32, 32), 32)
        wp[z, rows, :] = wf[rows, :].astype(BF16)
        return carry

    lax.fori_loop(0, BLK // 32, cast_rows, 0)
    wp[z, BLK:WROWS, :] = jnp.zeros((16, KV), BF16)
    wp[z, BLK:WROWS, 0:BLK] = jnp.broadcast_to(gain_row.astype(F32), (16, BLK)).astype(BF16)

    def wright(s):
        return remote(wp.at[z - s], wp.at[z - s], WL + s, dev(y, z + 1))

    def wleft(s):
        return remote(wp.at[z + s], wp.at[z + s], WR + s, dev(y, z - 1))

    @pl.when(z < 3)
    def _():
        wright(0).start()

    @pl.when(z > 0)
    def _():
        wleft(0).start()

    go(remote(wp.at[z], gos.at[2], GO + 2, (chip_rx, ry, f)))
    go(remote(wp.at[z], gos.at[0], GO + 0, (rx, (ry + 1) % 4, f)))
    go(remote(wp.at[z], gos.at[1], GO + 1, (rx, (ry + 3) % 4, f)))

    def far(zz):
        return remote(wp.at[zz], gos.at[3], GO + 3, (far_rx, ry, y * 4 + zz))

    loads[1].wait()

    def norm_rows(i, carry):
        rows = pl.ds(pl.multiple_of(i * 16, 16), 16)
        x = xv[rows, :].astype(F32)
        s = lax.rsqrt(jnp.sum(x * x, axis=1, keepdims=True) * (1.0 / 4096) + 1e-05)
        sc[rows, :] = jnp.broadcast_to(s, (16, 128))
        n = (x * s).astype(BF16)
        for yy in range(4):
            for b in range(4):
                at = yy * WIDE + b * BLK
                nown[yy, b, rows, :] = n[:, at:at + BLK]
        return carry

    lax.fori_loop(0, ROWS // 16, norm_rows, 0)

    remote(half(vg_hbm, 0, 0), half(vgp, 1, 0), VG + 0, ypeer(1)).wait_recv()
    go(remote(half(vgp, 1, 0), half(vgp, 2, 0), VG + 4, ypeer(1)))
    remote(half(vg_hbm, 0, 1), half(vgp, 3, 1), VG + 1, ypeer(3)).wait_recv()
    go(remote(half(vgp, 3, 1), half(vgp, 2, 1), VG + 5, ypeer(3)))

    upper = z // 2
    near = z + upper * (3 - 2 * z)

    def order(i):
        t = ((27 + 72 * near) // 4**i) % 4
        return t + upper * (3 - 2 * t)

    def slot(r):
        return pl.ds(r * ROWS, ROWS)

    def ncopy(i, r):
        b = order(i)
        return remote(nown.at[(y + r) % 4, b], npool.at[b, slot(r)], NS + 3 * i + r - 1, ypeer(r))

    for i in range(4):
        for r in (1, 3, 2):
            go(ncopy(i, r))

    def own_rows(i, carry):
        rows = pl.ds(pl.multiple_of(i * 64, 64), 64)
        for b in range(4):
            npool[b, rows, :] = nown[y, b, rows, :]
        return carry

    lax.fori_loop(0, ROWS // 64, own_rows, 0)

    def weights_arrive(s):
        @pl.when(z - s >= 0)
        def _():
            remote(wp.at[z - s], wp.at[z - s], WL + s - 1, dev(y, z)).wait_recv()

            @pl.when(z < 3)
            def _():
                wright(s).start()

        @pl.when(z + s <= 3)
        def _():
            remote(wp.at[z + s], wp.at[z + s], WR + s - 1, dev(y, z)).wait_recv()

            @pl.when(z > 0)
            def _():
                wleft(s).start()

        if s >= 2:
            @pl.when(z == 3)
            def _():
                far(3 - s).start()

            @pl.when(z == 0)
            def _():
                far(s).start()

    def rsright(b):
        return remote(rsend.at[b], rr.at[b], RR + b, dev(y, z + 1))

    def rsleft(b):
        return remote(rsend.at[b], rl.at[b], RL + b, dev(y, z - 1))

    def round_block(b, other=None):
        def rows_body(i, carry):
            rows = pl.ds(pl.multiple_of(i * 32, 32), 32)
            g = gbuf[b, rows, :]
            if other is not None:
                g = g + other[b, rows, :].astype(F32)
            rsend[b, rows, :] = g.astype(BF16)
            return carry

        lax.fori_loop(0, BLK // 32, rows_body, 0)

    def weight_grad(i):
        b = order(i)
        for r in (1, 3, 2):
            ncopy(i, r).wait_recv()
        npt[...] = npool[b].T

        def columns(c, carry):
            cols = pl.ds(pl.multiple_of(c * 256, 256), 256)
            gbuf[b, :, cols] = jnp.dot(npt[...], vgp[:, cols], preferred_element_type=F32)
            return carry

        lax.fori_loop(0, KV // 256, columns, 0)
        if i < 3:
            @pl.when(z == 0)
            def _():
                round_block(3 - i)
                rsright(3 - i).start()

            @pl.when(z == 3)
            def _():
                round_block(i)
                rsleft(i).start()

    def ucopy(i, r):
        b = order(i)
        return remote(us.at[b, slot(r)], ur.at[y, b], US + 3 * i + r - 1, ypeer(4 - r))

    def unit_grad(i):
        b = order(i)
        gl = wp[b, BLK:WROWS, 0:BLK].astype(F32)[0:1, :]

        def tokens(r, acc):
            rows = pl.ds(pl.multiple_of(r * ROWS, ROWS), ROWS)
            og = lax.dot_general(
                vgp[rows, :], wp[b, 0:BLK, :], (((1,), (1,)), ((), ())), preferred_element_type=F32
            )
            us[b, rows, :] = (og * gl).astype(BF16)
            prod = og * npool[b, rows, :].astype(F32)
            return acc + jnp.sum(prod.reshape(ROWS // 8, 8, BLK), axis=0)

        gg[b] = lax.fori_loop(0, 4, tokens, jnp.zeros((8, BLK), F32))
        for r in (1, 3, 2):
            go(ucopy(i, r))
        ur[y, b] = us[b, 0:ROWS, :]

    weights_arrive(1)
    loads[2].wait()
    for k, (s, h) in ((4, (2, 0)), (5, (2, 1)), (2, (1, 1)), (3, (3, 0))):
        remote(half(vgp, s, h), half(vgp, s, h), VG + k, ypeer(1)).wait_recv()
    weight_grad(0)
    weights_arrive(2)
    weight_grad(1)
    weight_grad(2)
    weights_arrive(3)

    def forward_right(b):
        remote(rsend.at[b], rr.at[b], RR + b, dev(y, z)).wait_recv()
        round_block(b, rr)
        rsright(b).start()

    def forward_left(b):
        remote(rsend.at[b], rl.at[b], RL + b, dev(y, z)).wait_recv()
        round_block(b, rl)
        rsleft(b).start()

    unit_grad(0)
    unit_grad(1)

    @pl.when(z == 1)
    def _():
        forward_right(3)

    @pl.when(z == 2)
    def _():
        forward_left(0)

    unit_grad(2)
    weight_grad(3)
    unit_grad(3)

    def ggcopy(d):
        zz = (z + d) % 4
        return remote(gg.at[zz], ggr.at[d - 1], GG + d - 1, dev(y, zz))

    for d in (1, 2, 3):
        go(ggcopy(d))

    @pl.when(z == 1)
    def _():
        forward_right(2)
        forward_left(0)

    @pl.when(z == 2)
    def _():
        forward_left(1)
        forward_right(3)

    total = (mix[0, 0, 0] + mix[0, 0, 1] + mix[0, 0, 2] + mix[0, 0, 3] + mix[0, 0, 4]).astype(F32)

    def share(n, width):
        return jnp.full((1, width), mix[0, 0, n].astype(F32), F32) / jnp.full((1, width), total, F32)

    from_chip, from_far = 2 - core, 1 + core

    for d in (1, 2, 3):
        ggcopy(d).wait_recv()
    g8 = gg[z] + ggr[0] + ggr[1] + ggr[2]
    grad_gain = jnp.sum(g8, axis=0, keepdims=True)
    own_gain = gain[0]
    new_gm = 0.9 * gain_m[0] + 0.1 * grad_gain
    new_gv = 0.999 * gain_v[0] + 0.001 * grad_gain * grad_gain
    ngm[0] = new_gm
    ngv[0] = new_gv
    stepped_g = own_gain - 0.01 * new_gm / (jnp.sqrt(new_gv) + 1e-08)

    remote(gos.at[2], gos.at[2], GO + 2, dev(y, z)).wait_recv()
    remote(gos.at[0], gos.at[0], GO + 0, dev(y, z)).wait_recv()
    remote(gos.at[1], gos.at[1], GO + 1, dev(y, z)).wait_recv()
    remote(gos.at[3], gos.at[3], GO + 3, dev(y, z)).wait_recv()

    def gossip_gain(n):
        return gos[n, BLK:WROWS, 0:BLK].astype(F32)[0:1, :]

    mixed_g = share(0, BLK) * stepped_g
    mixed_g = mixed_g + share(3, BLK) * gossip_gain(0) + share(4, BLK) * gossip_gain(1)
    mixed_g = mixed_g + share(from_chip, BLK) * gossip_gain(2) + share(from_far, BLK) * gossip_gain(3)
    ng[0] = mixed_g

    eye = lax.broadcasted_iota(jnp.int32, (BLK, BLK), 0) == lax.broadcasted_iota(jnp.int32, (BLK, BLK), 1)
    col = jnp.sum(jnp.where(eye, jnp.broadcast_to(gain_row.astype(F32), (BLK, BLK)), 0.0), axis=1, keepdims=True)
    gcol[...] = jnp.broadcast_to(col, (BLK, 128))

    def add_block(other):
        def rows_body(i, carry):
            rows = pl.ds(pl.multiple_of(i * 32, 32), 32)
            gbuf[z, rows, :] = gbuf[z, rows, :] + other[z, rows, :].astype(F32)
            return carry

        lax.fori_loop(0, BLK // 32, rows_body, 0)

    @pl.when(z > 0)
    def _():
        remote(rsend.at[z], rr.at[z], RR + z, dev(y, z)).wait_recv()
        add_block(rr)

    @pl.when(z < 3)
    def _():
        remote(rsend.at[z], rl.at[z], RL + z, dev(y, z)).wait_recv()
        add_block(rl)

    loads[3].wait()
    loads[4].wait()
    s0, s1, s2 = share(0, KV), share(3, KV), share(4, KV)
    s3, s4 = share(from_chip, KV), share(from_far, KV)

    def adam_rows(i, carry):
        rows = pl.ds(pl.multiple_of(i * 16, 16), 16)
        g = gcol[rows, 0:1] * gbuf[z, rows, :]
        new_m = 0.9 * mv[rows, :] + 0.1 * g
        new_v = 0.999 * vv[rows, :] + 0.001 * g * g
        nm[rows, :] = new_m
        nv[rows, :] = new_v
        own = wf[rows, :]
        stepped = own - 0.01 * (new_m / (jnp.sqrt(new_v) + 1e-08) + 0.1 * own)
        out = s0 * stepped + s1 * gos[0, rows, :].astype(F32) + s2 * gos[1, rows, :].astype(F32)
        nw[rows, :] = out + s3 * gos[2, rows, :].astype(F32) + s4 * gos[3, rows, :].astype(F32)
        return carry

    lax.fori_loop(0, BLK // 16, adam_rows, 0)

    for i in range(4):
        for r in (1, 3, 2):
            ucopy(i, r).wait_recv()

    def grad_rows(i, carry):
        rows = pl.ds(pl.multiple_of(i * 16, 16), 16)
        s = sc[rows, 0:1]
        inner = jnp.zeros((16, 1), F32)
        for yy in range(4):
            for b in range(4):
                at = yy * WIDE + b * BLK
                unit = xv[rows, at:at + BLK].astype(F32) * s
                inner = inner + jnp.sum(ur[yy, b, rows, :].astype(F32) * unit, axis=1, keepdims=True)
        inner = inner * (1.0 / 4096)
        for yy in range(4):
            for b in range(4):
                at = yy * WIDE + b * BLK
                unit = xv[rows, at:at + BLK].astype(F32) * s
                ig[rows, at:at + BLK] = s * (ur[yy, b, rows, :].astype(F32) - unit * inner)
        return carry

    lax.fori_loop(0, ROWS // 16, grad_rows, 0)

    for _, copy in sent:
        copy.wait_send()
    for s in range(3):
        @pl.when((z < 3) & (z - s >= 0))
        def _():
            wright(s).wait_send()

        @pl.when((z > 0) & (z + s <= 3))
        def _():
            wleft(s).wait_send()

    for s in (2, 3):
        @pl.when(z == 3)
        def _():
            far(3 - s).wait_send()

        @pl.when(z == 0)
        def _():
            far(s).wait_send()

    for b in range(4):
        @pl.when(z < b)
        def _():
            rsright(b).wait_send()

        @pl.when(z > b)
        def _():
            rsleft(b).wait_send()


def body(inputs, value_grad, weight, weight_m, weight_v, gain, gain_m, gain_v, mixing):
    vmem = pl.BlockSpec(memory_space=pltpu.VMEM)
    hbm = pl.BlockSpec(memory_space=pl.ANY)
    outs = pl.pallas_call(
        step_kernel,
        name="gossip_step",
        out_shape=[
            jax.ShapeDtypeStruct((ROWS, 4 * WIDE), F32),
            jax.ShapeDtypeStruct((BLK, KV), F32),
            jax.ShapeDtypeStruct((BLK, KV), F32),
            jax.ShapeDtypeStruct((BLK, KV), F32),
            jax.ShapeDtypeStruct((1, 1, BLK), F32),
            jax.ShapeDtypeStruct((1, 1, BLK), F32),
            jax.ShapeDtypeStruct((1, 1, BLK), F32),
        ],
        in_specs=[pl.BlockSpec(memory_space=pltpu.SMEM)] + [hbm] * 5 + [vmem] * 3,
        out_specs=[vmem] * 7,
        scratch_shapes=[
            pltpu.VMEM((ROWS, 4 * WIDE), BF16),
            pltpu.VMEM((BLK, KV), F32),
            pltpu.VMEM((BLK, KV), F32),
            pltpu.VMEM((BLK, KV), F32),
            pltpu.VMEM((4 * ROWS, KV), BF16),
            pltpu.VMEM((4, 4, ROWS, BLK), BF16),
            pltpu.VMEM((4, 4 * ROWS, BLK), BF16),
            pltpu.VMEM((BLK, 4 * ROWS), BF16),
            pltpu.VMEM((4, WROWS, KV), BF16),
            pltpu.VMEM((4, 4 * ROWS, BLK), BF16),
            pltpu.VMEM((4, 4, ROWS, BLK), BF16),
            pltpu.VMEM((4, BLK, KV), F32),
            pltpu.VMEM((4, BLK, KV), BF16),
            pltpu.VMEM((4, BLK, KV), BF16),
            pltpu.VMEM((4, BLK, KV), BF16),
            pltpu.VMEM((4, 8, BLK), F32),
            pltpu.VMEM((3, 8, BLK), F32),
            pltpu.VMEM((4, WROWS, KV), BF16),
            pltpu.VMEM((ROWS, 128), F32),
            pltpu.VMEM((BLK, 128), F32),
            pltpu.SemaphoreType.DMA((5,)),
            pltpu.SemaphoreType.DMA((NSEM,)),
            pltpu.SemaphoreType.DMA((NSEM,)),
        ],
        compiler_params=pltpu.CompilerParams(
            collective_id=0, has_side_effects=True, vmem_limit_bytes=56 << 20
        ),
    )(
        mixing,
        inputs.reshape(ROWS, 4 * WIDE),
        value_grad.reshape(ROWS, KV),
        weight[0, 0],
        weight_m[0, 0],
        weight_v[0, 0],
        gain,
        gain_m,
        gain_v,
    )
    ig, nw, nm, nv, ng, ngm, ngv = outs
    return (ig.reshape(inputs.shape), nw[None, None], nm[None, None], nv[None, None], ng, ngm, ngv)


def solution(mesh):
    placed = (
        P("rx", "ry", None, "fsdp", None),
        P("rx", "ry", None, "fsdp", None),
        P("rx", "ry", "fsdp", None),
        P("rx", "ry", "fsdp", None),
        P("rx", "ry", "fsdp", None),
        P("rx", "ry", "fsdp"),
        P("rx", "ry", "fsdp"),
        P("rx", "ry", "fsdp"),
        P("rx", "ry", None),
    )
    return jax.shard_map(
        body,
        mesh=mesh,
        in_specs=placed,
        out_specs=(
            P("rx", "ry", None, "fsdp", None),
            P("rx", "ry", "fsdp", None),
            P("rx", "ry", "fsdp", None),
            P("rx", "ry", "fsdp", None),
            P("rx", "ry", "fsdp"),
            P("rx", "ry", "fsdp"),
            P("rx", "ry", "fsdp"),
        ),
        check_vma=False,
    )
```

```python
import jax
import jax.numpy as jnp
from jax import lax
from jax.experimental import pallas as pl
from jax.experimental.pallas import tpu as pltpu
from jax.sharding import PartitionSpec as P

MESH = pl.DeviceIdType.MESH
F32 = jnp.float32
BF16 = jnp.bfloat16

ROWS = 256
BLK = 256
KV = 1024
WIDE = 1024
WROWS = BLK + 16

VG = 0
WL = 6
WR = 14
NS = 22
US = 34
RR = 46
RL = 54
GG = 62
GO = 65
NSEM = 70


def KC(k):
    for lo, c in ((65, "GO"), (62, "GG"), (46, "RS"), (34, "US"), (22, "NS"), (6, "W"), (0, "VG")):
        if k >= lo:
            return c


def step_kernel(
    mix, x_hbm, vg_hbm, w_hbm, m_hbm, v_hbm, gain, gain_m, gain_v,
    ur, nw, nm, nv, ng, ngm, ngv,
    xv, wf, mv, vv, vgp, nown, npool, npt, wp, us, gbuf, rsend, rr, rl, gg, ggr, gos, gcol,
    lsem, osem, ssem, rsem,
):
    rx = lax.axis_index("rx")
    ry = lax.axis_index("ry")
    f = lax.axis_index("fsdp")
    zh = rx // 2
    core = rx % 2
    y = f // 4
    z = f % 4

    def dev(yy, zz):
        return (rx, ry, yy * 4 + zz)

    def ypeer(r):
        return dev((y + r) % 4, z)

    far_rx = (1 - zh) * 2 + (1 - core)
    chip_rx = zh * 2 + (1 - core)

    def remote(src, dst, k, device):
        return pltpu.make_async_remote_copy(
            src_ref=src, dst_ref=dst, send_sem=ssem.at[k], recv_sem=rsem.at[k],
            device_id=device, device_id_type=MESH,
        )

    loads = [
        pltpu.make_async_copy(w_hbm, wf, lsem.at[0]),
        pltpu.make_async_copy(x_hbm, xv, lsem.at[1]),
        pltpu.make_async_copy(vg_hbm, vgp.at[pl.ds(0, ROWS)], lsem.at[2]),
        pltpu.make_async_copy(m_hbm, mv, lsem.at[3]),
        pltpu.make_async_copy(v_hbm, vv, lsem.at[4]),
    ]
    for c in loads:
        c.start()

    barrier = pltpu.get_barrier_semaphore()
    far_base = (1 - z // 2) * 2
    partners = [ypeer(1), ypeer(2), ypeer(3)]
    partners += [dev(y, (z + 1) % 4), dev(y, (z + 2) % 4), dev(y, (z + 3) % 4)]
    partners += [(rx, (ry + 1) % 4, f), (rx, (ry + 3) % 4, f), (chip_rx, ry, f)]
    partners += [(far_rx, ry, y * 4 + far_base), (far_rx, ry, y * 4 + far_base + 1)]
    for p in partners:
        pl.semaphore_signal(barrier, inc=1, device_id=p, device_id_type=MESH)
    pl.semaphore_wait(barrier, len(partners))

    sent = []

    def go(copy, cond=None):
        copy.start()
        sent.append((cond, copy))

    def half(ref, slot, h):
        return ref.at[pl.ds(slot * ROWS + h * (ROWS // 2), ROWS // 2)]

    go(remote(half(vg_hbm, 0, 0), half(vgp, 1, 0), VG + 0, ypeer(1)))
    go(remote(half(vg_hbm, 0, 1), half(vgp, 3, 1), VG + 1, ypeer(3)))
    go(remote(half(vg_hbm, 0, 1), half(vgp, 1, 1), VG + 2, ypeer(1)))
    go(remote(half(vg_hbm, 0, 0), half(vgp, 3, 0), VG + 3, ypeer(3)))

    loads[0].wait()
    gain_row = gain[0].astype(BF16)

    def cast_rows(i, carry):
        rows = pl.ds(pl.multiple_of(i * 32, 32), 32)
        wp[z, rows, :] = wf[rows, :].astype(BF16)
        return carry

    lax.fori_loop(0, BLK // 32, cast_rows, 0)
    wp[z, BLK:WROWS, :] = jnp.zeros((16, KV), BF16)
    wp[z, BLK:WROWS, 0:BLK] = jnp.broadcast_to(gain_row.astype(F32), (16, BLK)).astype(BF16)

    def whalf(block, h):
        return wp.at[block, pl.ds(h * 128, 128 + 16 * h)]

    def wright(s, h):
        return remote(whalf(z - s, h), whalf(z - s, h), WL + 2 * s + h, dev(y, z + 1))

    def wleft(s, h):
        return remote(whalf(z + s, h), whalf(z + s, h), WR + 2 * s + h, dev(y, z - 1))

    def from_left(s, h):
        remote(whalf(z - s, h), whalf(z - s, h), WL + 2 * s + h - 2, dev(y, z)).wait_recv()

    def from_right(s, h):
        remote(whalf(z + s, h), whalf(z + s, h), WR + 2 * s + h - 2, dev(y, z)).wait_recv()

    def far(zz, h):
        return remote(
            whalf(zz, h), gos.at[3, pl.ds(h * 128, 128 + 16 * h)], GO + 3 + h,
            (far_rx, ry, y * 4 + zz))

    @pl.when(z < 3)
    def _():
        wright(0, 0).start()

    @pl.when(z > 0)
    def _():
        wleft(0, 0).start()

    @pl.when(z < 2)
    def _():
        wright(0, 1).start()

    @pl.when(z > 1)
    def _():
        wleft(0, 1).start()

    go(remote(wp.at[z], gos.at[2], GO + 2, (chip_rx, ry, f)))
    go(remote(wp.at[z], gos.at[0], GO + 0, (rx, (ry + 1) % 4, f)))
    go(remote(wp.at[z], gos.at[1], GO + 1, (rx, (ry + 3) % 4, f)))

    loads[1].wait()

    def norm_rows(i, carry):
        rows = pl.ds(pl.multiple_of(i * 16, 16), 16)
        x = xv[rows, :].astype(F32)
        s = lax.rsqrt(jnp.sum(x * x, axis=1, keepdims=True) * (1.0 / 4096) + 1e-05)
        n = (x * s).astype(BF16)
        for yy in range(4):
            for b in range(4):
                at = yy * WIDE + b * BLK
                nown[yy, b, rows, :] = n[:, at:at + BLK]
        return carry

    lax.fori_loop(0, ROWS // 16, norm_rows, 0)

    remote(half(vg_hbm, 0, 0), half(vgp, 1, 0), VG + 0, ypeer(1)).wait_recv()
    go(remote(half(vgp, 1, 0), half(vgp, 2, 0), VG + 4, ypeer(1)))
    remote(half(vg_hbm, 0, 1), half(vgp, 3, 1), VG + 1, ypeer(3)).wait_recv()
    go(remote(half(vgp, 3, 1), half(vgp, 2, 1), VG + 5, ypeer(3)))

    @pl.when(z == 2)
    def _():
        from_left(1, 0)
        wright(1, 0).start()

    @pl.when(z == 1)
    def _():
        from_right(1, 0)
        wleft(1, 0).start()

    upper = z // 2
    near = z + upper * (3 - 2 * z)

    def order(i):
        t = ((27 + 72 * near) // 4**i) % 4
        return t + upper * (3 - 2 * t)

    def slot(r):
        return pl.ds(r * ROWS, ROWS)

    def ncopy(i, r):
        b = order(i)
        return remote(nown.at[(y + r) % 4, b], npool.at[b, slot(r)], NS + 3 * i + r - 1, ypeer(r))

    for i in range(4):
        for r in (1, 3, 2):
            go(ncopy(i, r))

    def own_rows(i, carry):
        rows = pl.ds(pl.multiple_of(i * 64, 64), 64)
        for b in range(4):
            npool[b, rows, :] = nown[y, b, rows, :]
        return carry

    lax.fori_loop(0, ROWS // 64, own_rows, 0)

    def half_rows(h):
        return pl.ds(h * 128, 128)

    def rsright(b, h):
        return remote(rsend.at[b, half_rows(h)], rr.at[b, half_rows(h)], RR + 2 * b + h, dev(y, z + 1))

    def rsleft(b, h):
        return remote(rsend.at[b, half_rows(h)], rl.at[b, half_rows(h)], RL + 2 * b + h, dev(y, z - 1))

    def round_half(b, h, other=None):
        def rows_body(i, carry):
            rows = pl.ds(pl.multiple_of(h * 128 + i * 32, 32), 32)
            g = gbuf[b, rows, :]
            if other is not None:
                g = g + other[b, rows, :].astype(F32)
            rsend[b, rows, :] = g.astype(BF16)
            return carry

        lax.fori_loop(0, 4, rows_body, 0)

    def weight_grad(i):
        b = order(i)
        for r in (1, 3, 2):
            ncopy(i, r).wait_recv()
        npt[...] = npool[b].T

        def columns(c, carry):
            cols = pl.ds(pl.multiple_of(c * 256, 256), 256)
            gbuf[b, :, cols] = jnp.dot(npt[...], vgp[:, cols], preferred_element_type=F32)
            return carry

        lax.fori_loop(0, KV // 256, columns, 0)
        if i < 3:
            @pl.when(z == 0)
            def _():
                for h in (0, 1):
                    round_half(3 - i, h)
                    rsright(3 - i, h).start()

            @pl.when(z == 3)
            def _():
                for h in (0, 1):
                    round_half(i, h)
                    rsleft(i, h).start()

    def ucopy(i, r):
        b = order(i)
        return remote(us.at[b, slot(r)], ur.at[y, b], US + 3 * i + r - 1, ypeer(4 - r))

    def own_ur(i):
        b = order(i)
        return pltpu.make_async_copy(us.at[b, slot(0)], ur.at[y, b], osem.at[3 + i])

    def unit_grad(i):
        b = order(i)
        gl = wp[b, BLK:WROWS, 0:BLK].astype(F32)[0:1, :]

        def tokens(r, acc):
            rows = pl.ds(pl.multiple_of(r * ROWS, ROWS), ROWS)
            og = lax.dot_general(
                vgp[rows, :], wp[b, 0:BLK, :], (((1,), (1,)), ((), ())), preferred_element_type=F32
            )
            us[b, rows, :] = (og * gl).astype(BF16)
            prod = og * npool[b, rows, :].astype(F32)
            return acc + jnp.sum(prod.reshape(ROWS // 8, 8, BLK), axis=0)

        gg[b] = lax.fori_loop(0, 4, tokens, jnp.zeros((8, BLK), F32))
        for r in (1, 3, 2):
            go(ucopy(i, r))
        own_ur(i).start()

    def relay_right(s):
        for h in (0, 1):
            from_left(s, h)
            wright(s, h).start()

    def relay_left(s):
        for h in (0, 1):
            from_right(s, h)
            wleft(s, h).start()

    @pl.when(z == 2)
    def _():
        from_left(1, 1)
        wright(1, 1).start()
        wright(0, 1).start()
        relay_left(1)

    @pl.when(z == 1)
    def _():
        from_right(1, 1)
        wleft(1, 1).start()
        wleft(0, 1).start()
        relay_right(1)

    def gossip_out(s, h):
        @pl.when(z == 3)
        def _():
            from_left(s, h)
            far(3 - s, h).start()

        @pl.when(z == 0)
        def _():
            from_right(s, h)
            far(s, h).start()

    def forward_right(b, h):
        remote(rsend.at[b, half_rows(h)], rr.at[b, half_rows(h)], RR + 2 * b + h, dev(y, z)).wait_recv()
        round_half(b, h, rr)
        rsright(b, h).start()

    def forward_left(b, h):
        remote(rsend.at[b, half_rows(h)], rl.at[b, half_rows(h)], RL + 2 * b + h, dev(y, z)).wait_recv()
        round_half(b, h, rl)
        rsleft(b, h).start()

    def forward_first(h):
        @pl.when(z == 1)
        def _():
            forward_right(3, h)

        @pl.when(z == 2)
        def _():
            forward_left(0, h)

    def forward_second(h):
        @pl.when(z == 1)
        def _():
            forward_left(0, h)
            forward_right(2, h)

        @pl.when(z == 2)
        def _():
            forward_right(3, h)
            forward_left(1, h)

    gossip_out(2, 0)
    loads[2].wait()
    for k, (s, h) in ((4, (2, 0)), (5, (2, 1)), (2, (1, 1)), (3, (3, 0))):
        remote(half(vgp, s, h), half(vgp, s, h), VG + k, ypeer(1)).wait_recv()
    gossip_out(2, 1)
    weight_grad(0)

    @pl.when(z == 2)
    def _():
        relay_right(2)

    @pl.when(z == 1)
    def _():
        relay_left(2)

    weight_grad(1)
    forward_first(0)
    weight_grad(2)
    gossip_out(3, 0)
    gossip_out(3, 1)

    @pl.when(z == 3)
    def _():
        from_left(1, 0)
        from_left(1, 1)

    @pl.when(z == 0)
    def _():
        from_right(1, 0)
        from_right(1, 1)

    unit_grad(0)
    forward_first(1)
    unit_grad(1)
    unit_grad(2)
    weight_grad(3)
    forward_second(0)
    unit_grad(3)

    def ggcopy(d):
        zz = (z + d) % 4
        return remote(gg.at[zz], ggr.at[d - 1], GG + d - 1, dev(y, zz))

    for d in (1, 2, 3):
        go(ggcopy(d))

    forward_second(1)

    total = (mix[0, 0, 0] + mix[0, 0, 1] + mix[0, 0, 2] + mix[0, 0, 3] + mix[0, 0, 4]).astype(F32)

    def share(n, width):
        return jnp.full((1, width), mix[0, 0, n].astype(F32), F32) / jnp.full((1, width), total, F32)

    from_chip, from_far = 2 - core, 1 + core

    for d in (1, 2, 3):
        ggcopy(d).wait_recv()
    g8 = gg[z] + ggr[0] + ggr[1] + ggr[2]
    grad_gain = jnp.sum(g8, axis=0, keepdims=True)
    own_gain = gain[0]
    new_gm = 0.9 * gain_m[0] + 0.1 * grad_gain
    new_gv = 0.999 * gain_v[0] + 0.001 * grad_gain * grad_gain
    ngm[0] = new_gm
    ngv[0] = new_gv
    stepped_g = own_gain - 0.01 * new_gm / (jnp.sqrt(new_gv) + 1e-08)

    remote(gos.at[2], gos.at[2], GO + 2, dev(y, z)).wait_recv()
    remote(gos.at[0], gos.at[0], GO + 0, dev(y, z)).wait_recv()
    remote(gos.at[1], gos.at[1], GO + 1, dev(y, z)).wait_recv()
    far_in = gos.at[3, pl.ds(0, 128)]
    remote(far_in, far_in, GO + 3, dev(y, z)).wait_recv()
    far_in = gos.at[3, pl.ds(128, 144)]
    remote(far_in, far_in, GO + 4, dev(y, z)).wait_recv()

    def gossip_gain(n):
        return gos[n, BLK:WROWS, 0:BLK].astype(F32)[0:1, :]

    mixed_g = share(0, BLK) * stepped_g
    mixed_g = mixed_g + share(3, BLK) * gossip_gain(0) + share(4, BLK) * gossip_gain(1)
    mixed_g = mixed_g + share(from_chip, BLK) * gossip_gain(2) + share(from_far, BLK) * gossip_gain(3)
    ng[0] = mixed_g

    eye = lax.broadcasted_iota(jnp.int32, (BLK, BLK), 0) == lax.broadcasted_iota(jnp.int32, (BLK, BLK), 1)
    col = jnp.sum(jnp.where(eye, jnp.broadcast_to(gain_row.astype(F32), (BLK, BLK)), 0.0), axis=1, keepdims=True)
    gcol[...] = jnp.broadcast_to(col, (BLK, 128))

    @pl.when(z == 0)
    def _():
        rr[z] = jnp.zeros((BLK, KV), BF16)

    @pl.when(z == 3)
    def _():
        rl[z] = jnp.zeros((BLK, KV), BF16)

    loads[3].wait()
    loads[4].wait()
    s0, s1, s2 = share(0, KV), share(3, KV), share(4, KV)
    s3, s4 = share(from_chip, KV), share(from_far, KV)

    def adam_rows(i, carry):
        rows = pl.ds(pl.multiple_of(i * 16, 16), 16)
        g = gbuf[z, rows, :] + rr[z, rows, :].astype(F32) + rl[z, rows, :].astype(F32)
        g = gcol[rows, 0:1] * g
        new_m = 0.9 * mv[rows, :] + 0.1 * g
        new_v = 0.999 * vv[rows, :] + 0.001 * g * g
        mv[rows, :] = new_m
        vv[rows, :] = new_v
        own = wf[rows, :]
        stepped = own - 0.01 * (new_m / (jnp.sqrt(new_v) + 1e-08) + 0.1 * own)
        out = s0 * stepped + s1 * gos[0, rows, :].astype(F32) + s2 * gos[1, rows, :].astype(F32)
        wf[rows, :] = out + s3 * gos[2, rows, :].astype(F32) + s4 * gos[3, rows, :].astype(F32)
        return carry

    for h in (0, 1):
        @pl.when(z > 0)
        def _():
            remote(rsend.at[z, half_rows(h)], rr.at[z, half_rows(h)], RR + 2 * z + h, dev(y, z)).wait_recv()

        @pl.when(z < 3)
        def _():
            remote(rsend.at[z, half_rows(h)], rl.at[z, half_rows(h)], RL + 2 * z + h, dev(y, z)).wait_recv()

        lax.fori_loop(8 * h, 8 * h + 8, adam_rows, 0)

    writes = [
        pltpu.make_async_copy(wf, nw, osem.at[0]),
        pltpu.make_async_copy(mv, nm, osem.at[1]),
        pltpu.make_async_copy(vv, nv, osem.at[2]),
    ]
    for c in writes:
        c.start()

    for i in range(4):
        for r in (1, 3, 2):
            ucopy(i, r).wait_recv()
        own_ur(i).wait()
    for c in writes:
        c.wait()

    for _, copy in sent:
        copy.wait_send()
    for h in (0, 1):
        for s, right, left in (
            (0, z < 3, z > 0),
            (1, (z == 1) | (z == 2), (z == 1) | (z == 2)),
            (2, z == 2, z == 1),
        ):
            @pl.when(right)
            def _():
                wright(s, h).wait_send()

            @pl.when(left)
            def _():
                wleft(s, h).wait_send()

        for s in (2, 3):
            @pl.when(z == 3)
            def _():
                far(3 - s, h).wait_send()

            @pl.when(z == 0)
            def _():
                far(s, h).wait_send()

        for b in range(4):
            @pl.when(z < b)
            def _():
                rsright(b, h).wait_send()

            @pl.when(z > b)
            def _():
                rsleft(b, h).wait_send()


def finish_kernel(x, ur, nw, nm, nv, ng, ngm, ngv, ig, nw_out, nm_out, nv_out, ng_out, ngm_out, ngv_out):
    nw_out[...] = nw[...]
    nm_out[...] = nm[...]
    nv_out[...] = nv[...]
    ng_out[...] = ng[...]
    ngm_out[...] = ngm[...]
    ngv_out[...] = ngv[...]

    def grad_rows(i, carry):
        rows = pl.ds(pl.multiple_of(i * 16, 16), 16)
        own = x[rows, :].astype(F32)
        s = lax.rsqrt(jnp.sum(own * own, axis=1, keepdims=True) * (1.0 / 4096) + 1e-05)
        inner = jnp.zeros((16, BLK), F32)
        for yy in range(4):
            for b in range(4):
                at = yy * WIDE + b * BLK
                inner = inner + ur[yy, b, rows, :].astype(F32) * (own[:, at:at + BLK] * s)
        inner = jnp.sum(inner, axis=1, keepdims=True) * (1.0 / 4096)
        for yy in range(4):
            for b in range(4):
                at = yy * WIDE + b * BLK
                unit = own[:, at:at + BLK] * s
                ig[rows, at:at + BLK] = s * (ur[yy, b, rows, :].astype(F32) - unit * inner)
        return carry

    lax.fori_loop(0, x.shape[0] // 16, grad_rows, 0)


def body(inputs, value_grad, weight, weight_m, weight_v, gain, gain_m, gain_v, mixing):
    vmem = pl.BlockSpec(memory_space=pltpu.VMEM)
    hbm = pl.BlockSpec(memory_space=pl.ANY)
    tokens = inputs.reshape(ROWS, 4 * WIDE)
    weights = [jax.ShapeDtypeStruct((BLK, KV), F32)] * 3
    gains = [jax.ShapeDtypeStruct((1, 1, BLK), F32)] * 3
    parts = pl.pallas_call(
        step_kernel,
        name="gossip_step",
        out_shape=[jax.ShapeDtypeStruct((4, 4, ROWS, BLK), BF16)] + weights + gains,
        in_specs=[pl.BlockSpec(memory_space=pltpu.SMEM)] + [hbm] * 5 + [vmem] * 3,
        out_specs=[hbm] * 4 + [vmem] * 3,
        scratch_shapes=[
            pltpu.VMEM((ROWS, 4 * WIDE), BF16),
            pltpu.VMEM((BLK, KV), F32),
            pltpu.VMEM((BLK, KV), F32),
            pltpu.VMEM((BLK, KV), F32),
            pltpu.VMEM((4 * ROWS, KV), BF16),
            pltpu.VMEM((4, 4, ROWS, BLK), BF16),
            pltpu.VMEM((4, 4 * ROWS, BLK), BF16),
            pltpu.VMEM((BLK, 4 * ROWS), BF16),
            pltpu.VMEM((4, WROWS, KV), BF16),
            pltpu.VMEM((4, 4 * ROWS, BLK), BF16),
            pltpu.VMEM((4, BLK, KV), F32),
            pltpu.VMEM((4, BLK, KV), BF16),
            pltpu.VMEM((4, BLK, KV), BF16),
            pltpu.VMEM((4, BLK, KV), BF16),
            pltpu.VMEM((4, 8, BLK), F32),
            pltpu.VMEM((3, 8, BLK), F32),
            pltpu.VMEM((4, WROWS, KV), BF16),
            pltpu.VMEM((BLK, 128), F32),
            pltpu.SemaphoreType.DMA((5,)),
            pltpu.SemaphoreType.DMA((7,)),
            pltpu.SemaphoreType.DMA((NSEM,)),
            pltpu.SemaphoreType.DMA((NSEM,)),
        ],
        compiler_params=pltpu.CompilerParams(
            collective_id=0, has_side_effects=True, vmem_limit_bytes=60 << 20
        ),
    )(
        mixing,
        tokens,
        value_grad.reshape(ROWS, KV),
        weight[0, 0],
        weight_m[0, 0],
        weight_v[0, 0],
        gain,
        gain_m,
        gain_v,
    )
    steps = 4
    wide_block = pl.BlockSpec((ROWS // steps, 4 * WIDE), lambda i: (i, 0))
    row_block = pl.BlockSpec((BLK // steps, KV), lambda i: (i, 0))
    gain_block = pl.BlockSpec((1, 1, BLK), lambda i: (0, 0, 0))
    ig, nw, nm, nv, ng, ngm, ngv = pl.pallas_call(
        finish_kernel,
        name="finish",
        grid=(steps,),
        out_shape=[jax.ShapeDtypeStruct((ROWS, 4 * WIDE), F32)] + weights + gains,
        in_specs=[wide_block, pl.BlockSpec((4, 4, ROWS // steps, BLK), lambda i: (0, 0, i, 0))]
        + [row_block] * 3 + [gain_block] * 3,
        out_specs=[wide_block] + [row_block] * 3 + [gain_block] * 3,
        compiler_params=pltpu.CompilerParams(vmem_limit_bytes=60 << 20),
    )(tokens, *parts)
    return (ig.reshape(inputs.shape), nw[None, None], nm[None, None], nv[None, None], ng, ngm, ngv)


def solution(mesh):
    placed = (
        P("rx", "ry", None, "fsdp", None),
        P("rx", "ry", None, "fsdp", None),
        P("rx", "ry", "fsdp", None),
        P("rx", "ry", "fsdp", None),
        P("rx", "ry", "fsdp", None),
        P("rx", "ry", "fsdp"),
        P("rx", "ry", "fsdp"),
        P("rx", "ry", "fsdp"),
        P("rx", "ry", None),
    )
    return jax.shard_map(
        body,
        mesh=mesh,
        in_specs=placed,
        out_specs=(
            P("rx", "ry", None, "fsdp", None),
            P("rx", "ry", "fsdp", None),
            P("rx", "ry", "fsdp", None),
            P("rx", "ry", "fsdp", None),
            P("rx", "ry", "fsdp"),
            P("rx", "ry", "fsdp"),
            P("rx", "ry", "fsdp"),
        ),
        check_vma=False,
    )
```

```python
import jax
import jax.numpy as jnp
from jax import lax
from jax.experimental import pallas as pl
from jax.experimental.pallas import tpu as pltpu
from jax.sharding import PartitionSpec as P

MESH = pl.DeviceIdType.MESH
F32 = jnp.float32
BF16 = jnp.bfloat16

ROWS = 256
BLK = 256
KV = 1024
WIDE = 1024
WROWS = BLK + 16

VG = 0
WL = 6
WR = 14
NS = 22
US = 34
RR = 46
RL = 54
GG = 62
GO = 65
NSEM = 70


def KC(k):
    for lo, c in ((65, "GO"), (62, "GG"), (46, "RS"), (34, "US"), (22, "NS"), (6, "W"), (0, "VG")):
        if k >= lo:
            return c


def mirrored(z, codes, i):
    upper = z // 2
    near = z + upper * (3 - 2 * z)
    t = ((codes[0] + (codes[1] - codes[0]) * near) // 4**i) % 4
    return t + upper * (3 - 2 * t)


def grad_order(z, i):
    return mirrored(z, (27, 99), i)


def unit_order(z, i):
    return mirrored(z, (216, 225), i)


def step_kernel(
    mix, x_hbm, vg_hbm, w_hbm, m_hbm, v_hbm, gain, gain_m, gain_v,
    ur0, ur1, ur2, ur3, xv, sc, acc, nw, nm, nv, ng, ngm, ngv,
    wf, mv, vv, vgp, nown, npool, npt, wp, us, gbuf, rsend, rr, rl, gg, ggr, gos, gcol,
    lsem, ssem, rsem,
):
    ur = (ur0, ur1, ur2, ur3)
    rx = lax.axis_index("rx")
    ry = lax.axis_index("ry")
    f = lax.axis_index("fsdp")
    zh = rx // 2
    core = rx % 2
    y = f // 4
    z = f % 4

    def dev(yy, zz):
        return (rx, ry, yy * 4 + zz)

    def ypeer(r):
        return dev((y + r) % 4, z)

    far_rx = (1 - zh) * 2 + (1 - core)
    chip_rx = zh * 2 + (1 - core)

    def remote(src, dst, k, device):
        return pltpu.make_async_remote_copy(
            src_ref=src, dst_ref=dst, send_sem=ssem.at[k], recv_sem=rsem.at[k],
            device_id=device, device_id_type=MESH,
        )

    barrier = pltpu.get_barrier_semaphore()
    far_base = (1 - z // 2) * 2
    partners = [ypeer(1), ypeer(2), ypeer(3)]
    partners += [dev(y, (z + 1) % 4), dev(y, (z + 2) % 4), dev(y, (z + 3) % 4)]
    partners += [(rx, (ry + 1) % 4, f), (rx, (ry + 3) % 4, f), (chip_rx, ry, f)]
    partners += [(far_rx, ry, y * 4 + far_base), (far_rx, ry, y * 4 + far_base + 1)]
    for p in partners:
        pl.semaphore_signal(barrier, inc=1, device_id=p, device_id_type=MESH)
    loads = [
        pltpu.make_async_copy(w_hbm, wf, lsem.at[0]),
        pltpu.make_async_copy(x_hbm, xv, lsem.at[1]),
        pltpu.make_async_copy(vg_hbm, vgp.at[pl.ds(0, ROWS)], lsem.at[2]),
        pltpu.make_async_copy(m_hbm, mv, lsem.at[3]),
        pltpu.make_async_copy(v_hbm, vv, lsem.at[4]),
    ]
    for c in loads:
        c.start()

    pl.semaphore_wait(barrier, len(partners))

    sent = []

    def go(copy, cond=None):
        copy.start()
        sent.append((cond, copy))

    def half(ref, slot, h):
        return ref.at[pl.ds(slot * ROWS + h * (ROWS // 2), ROWS // 2)]

    go(remote(half(vg_hbm, 0, 0), half(vgp, 1, 0), VG + 0, ypeer(1)))
    go(remote(half(vg_hbm, 0, 1), half(vgp, 3, 1), VG + 1, ypeer(3)))
    go(remote(half(vg_hbm, 0, 1), half(vgp, 1, 1), VG + 2, ypeer(1)))
    go(remote(half(vg_hbm, 0, 0), half(vgp, 3, 0), VG + 3, ypeer(3)))

    loads[0].wait()
    gain_row = gain[0].astype(BF16)

    def cast_rows(i, carry):
        rows = pl.ds(pl.multiple_of(i * 32, 32), 32)
        wp[z, rows, :] = wf[rows, :].astype(BF16)
        return carry

    lax.fori_loop(0, BLK // 32, cast_rows, 0)
    wp[z, BLK:WROWS, :] = jnp.zeros((16, KV), BF16)
    wp[z, BLK:WROWS, 0:BLK] = jnp.broadcast_to(gain_row.astype(F32), (16, BLK)).astype(BF16)

    def whalf(block, h):
        return wp.at[block, pl.ds(h * 128, 128 + 16 * h)]

    def wright(s, h):
        return remote(whalf(z - s, h), whalf(z - s, h), WL + 2 * s + h, dev(y, z + 1))

    def wleft(s, h):
        return remote(whalf(z + s, h), whalf(z + s, h), WR + 2 * s + h, dev(y, z - 1))

    def from_left(s, h):
        remote(whalf(z - s, h), whalf(z - s, h), WL + 2 * s + h - 2, dev(y, z)).wait_recv()

    def from_right(s, h):
        remote(whalf(z + s, h), whalf(z + s, h), WR + 2 * s + h - 2, dev(y, z)).wait_recv()

    def far(zz, h):
        return remote(
            whalf(zz, h), gos.at[3, pl.ds(h * 128, 128 + 16 * h)], GO + 3 + h,
            (far_rx, ry, y * 4 + zz))

    @pl.when(z < 3)
    def _():
        wright(0, 0).start()

    @pl.when(z > 0)
    def _():
        wleft(0, 0).start()

    @pl.when(z < 2)
    def _():
        wright(0, 1).start()

    @pl.when(z > 1)
    def _():
        wleft(0, 1).start()

    go(remote(wp.at[z], gos.at[2], GO + 2, (chip_rx, ry, f)))
    go(remote(wp.at[z], gos.at[0], GO + 0, (rx, (ry + 1) % 4, f)))
    go(remote(wp.at[z], gos.at[1], GO + 1, (rx, (ry + 3) % 4, f)))

    loads[1].wait()

    def norm_rows(i, carry):
        rows = pl.ds(pl.multiple_of(i * 64, 64), 64)
        part = jnp.zeros((64, 128), F32)
        for c in range(4 * WIDE // 128):
            x = xv[rows, c * 128:(c + 1) * 128].astype(F32)
            part = part + x * x
        s = lax.rsqrt(jnp.sum(part, axis=1, keepdims=True) * (1.0 / 4096) + 1e-05)
        s = jnp.broadcast_to(s, (64, 128))
        sc[rows, :] = s
        for yy in range(4):
            for b in range(4):
                for c in (0, 128):
                    at = yy * WIDE + b * BLK + c
                    nown[yy, b, rows, c:c + 128] = (xv[rows, at:at + 128].astype(F32) * s).astype(BF16)
        return carry

    lax.fori_loop(0, ROWS // 64, norm_rows, 0)

    remote(half(vg_hbm, 0, 0), half(vgp, 1, 0), VG + 0, ypeer(1)).wait_recv()
    go(remote(half(vgp, 1, 0), half(vgp, 2, 0), VG + 4, ypeer(1)))
    remote(half(vg_hbm, 0, 1), half(vgp, 3, 1), VG + 1, ypeer(3)).wait_recv()
    go(remote(half(vgp, 3, 1), half(vgp, 2, 1), VG + 5, ypeer(3)))

    @pl.when(z == 2)
    def _():
        from_left(1, 0)
        wright(1, 0).start()

    @pl.when(z == 1)
    def _():
        from_right(1, 0)
        wleft(1, 0).start()

    def order(i):
        return grad_order(z, i)

    def slot(r):
        return pl.ds(r * ROWS, ROWS)

    def ncopy(i, r):
        b = order(i)
        return remote(nown.at[(y + r) % 4, b], npool.at[b, slot(r)], NS + 3 * i + r - 1, ypeer(r))

    for i in range(4):
        for r in (1, 3, 2):
            go(ncopy(i, r))

    def own_rows(i, carry):
        rows = pl.ds(pl.multiple_of(i * 64, 64), 64)
        for b in range(4):
            npool[b, rows, :] = nown[y, b, rows, :]
        return carry

    lax.fori_loop(0, ROWS // 64, own_rows, 0)

    def half_rows(h):
        return pl.ds(h * 128, 128)

    def rsright(b, h):
        return remote(rsend.at[b, half_rows(h)], rr.at[b, half_rows(h)], RR + 2 * b + h, dev(y, z + 1))

    def rsleft(b, h):
        return remote(rsend.at[b, half_rows(h)], rl.at[b, half_rows(h)], RL + 2 * b + h, dev(y, z - 1))

    def round_half(b, h, other=None):
        def rows_body(i, carry):
            rows = pl.ds(pl.multiple_of(h * 128 + i * 32, 32), 32)
            g = gbuf[b, rows, :]
            if other is not None:
                g = g + other[b, rows, :].astype(F32)
            rsend[b, rows, :] = g.astype(BF16)
            return carry

        lax.fori_loop(0, 4, rows_body, 0)

    def weight_grad(i):
        b = order(i)
        for r in (1, 3, 2):
            ncopy(i, r).wait_recv()
        npt[...] = npool[b].T

        def columns(c, carry):
            cols = pl.ds(pl.multiple_of(c * 256, 256), 256)
            gbuf[b, :, cols] = jnp.dot(npt[...], vgp[:, cols], preferred_element_type=F32)
            return carry

        lax.fori_loop(0, KV // 256, columns, 0)
        if i < 3:
            @pl.when(z == 0)
            def _():
                for h in (0, 1):
                    round_half(3 - i, h)
                    rsright(3 - i, h).start()

            @pl.when(z == 3)
            def _():
                for h in (0, 1):
                    round_half(i, h)
                    rsleft(i, h).start()

    def ucopy(i, r):
        b = unit_order(z, i)
        return remote(us.at[b, slot(r)], ur[i].at[y], US + 3 * i + r - 1, ypeer(4 - r))

    def unit_grad(i):
        b = unit_order(z, i)
        gl = wp[b, BLK:WROWS, 0:BLK].astype(F32)[0:1, :]

        def tokens(r, carry):
            rows = pl.ds(pl.multiple_of(r * ROWS, ROWS), ROWS)
            og = lax.dot_general(
                vgp[rows, :], wp[b, 0:BLK, :], (((1,), (1,)), ((), ())), preferred_element_type=F32
            )
            us[b, rows, :] = (og * gl).astype(BF16)
            return carry

        lax.fori_loop(0, 4, tokens, 0)
        for r in (1, 3, 2):
            go(ucopy(i, r))
        ur[i][y] = us[b, 0:ROWS, :]

    eye = lax.broadcasted_iota(jnp.int32, (BLK, BLK), 0) == lax.broadcasted_iota(jnp.int32, (BLK, BLK), 1)

    def gain_grad(b):
        def rows_body(i, carry):
            rows = pl.ds(pl.multiple_of(i * 64, 64), 64)
            part = jnp.zeros((64, 128), F32)
            for c in range(KV // 128):
                cols = pl.ds(c * 128, 128)
                part = part + wp[b, rows, cols].astype(F32) * gbuf[b, rows, cols]
            gcol[rows, :] = part
            return carry

        lax.fori_loop(0, BLK // 64, rows_body, 0)
        col = jnp.sum(gcol[...], axis=1, keepdims=True)
        spread = jnp.where(eye, jnp.broadcast_to(col, (BLK, BLK)), 0.0)
        gg[b] = jnp.sum(spread.reshape(BLK // 8, 8, BLK), axis=0)

    def relay_right(s):
        for h in (0, 1):
            from_left(s, h)
            wright(s, h).start()

    def relay_left(s):
        for h in (0, 1):
            from_right(s, h)
            wleft(s, h).start()

    @pl.when(z == 2)
    def _():
        from_left(1, 1)
        wright(1, 1).start()
        wright(0, 1).start()
        relay_left(1)

    @pl.when(z == 1)
    def _():
        from_right(1, 1)
        wleft(1, 1).start()
        wleft(0, 1).start()
        relay_right(1)

    def gossip_out(s, h):
        @pl.when(z == 3)
        def _():
            from_left(s, h)
            far(3 - s, h).start()

        @pl.when(z == 0)
        def _():
            from_right(s, h)
            far(s, h).start()

    def forward_right(b, h):
        remote(rsend.at[b, half_rows(h)], rr.at[b, half_rows(h)], RR + 2 * b + h, dev(y, z)).wait_recv()
        round_half(b, h, rr)
        rsright(b, h).start()

    def forward_left(b, h):
        remote(rsend.at[b, half_rows(h)], rl.at[b, half_rows(h)], RL + 2 * b + h, dev(y, z)).wait_recv()
        round_half(b, h, rl)
        rsleft(b, h).start()

    def forward_first(h):
        @pl.when(z == 1)
        def _():
            forward_right(3, h)

        @pl.when(z == 2)
        def _():
            forward_left(0, h)

    def forward_second(h):
        @pl.when(z == 1)
        def _():
            forward_left(0, h)
            forward_right(2, h)

        @pl.when(z == 2)
        def _():
            forward_right(3, h)
            forward_left(1, h)

    gossip_out(2, 0)
    loads[2].wait()
    for k, (s, h) in ((4, (2, 0)), (5, (2, 1)), (2, (1, 1)), (3, (3, 0))):
        remote(half(vgp, s, h), half(vgp, s, h), VG + k, ypeer(1)).wait_recv()
    gossip_out(2, 1)
    unit_grad(0)
    weight_grad(0)

    @pl.when(z == 2)
    def _():
        relay_right(2)

    @pl.when(z == 1)
    def _():
        relay_left(2)

    unit_grad(1)
    weight_grad(1)
    forward_first(0)

    @pl.when(z == 3)
    def _():
        from_left(1, 0)
        from_left(1, 1)

    @pl.when(z == 0)
    def _():
        from_right(1, 0)
        from_right(1, 1)

    unit_grad(2)
    weight_grad(2)
    gossip_out(3, 0)
    gossip_out(3, 1)
    forward_first(1)
    unit_grad(3)
    weight_grad(3)
    forward_second(0)

    def gain_block(b, carry):
        gain_grad(b)
        return carry

    lax.fori_loop(0, 4, gain_block, 0)

    def ggcopy(d):
        zz = (z + d) % 4
        return remote(gg.at[zz], ggr.at[d - 1], GG + d - 1, dev(y, zz))

    for d in (1, 2, 3):
        go(ggcopy(d))

    forward_second(1)

    total = (mix[0, 0, 0] + mix[0, 0, 1] + mix[0, 0, 2] + mix[0, 0, 3] + mix[0, 0, 4]).astype(F32)

    def share(n, width):
        return jnp.full((1, width), mix[0, 0, n].astype(F32), F32) / jnp.full((1, width), total, F32)

    from_chip, from_far = 2 - core, 1 + core

    for d in (1, 2, 3):
        ggcopy(d).wait_recv()
    g8 = gg[z] + ggr[0] + ggr[1] + ggr[2]
    grad_gain = jnp.sum(g8, axis=0, keepdims=True)
    own_gain = gain[0]
    new_gm = 0.9 * gain_m[0] + 0.1 * grad_gain
    new_gv = 0.999 * gain_v[0] + 0.001 * grad_gain * grad_gain
    ngm[0] = new_gm
    ngv[0] = new_gv
    stepped_g = own_gain - 0.01 * new_gm / (jnp.sqrt(new_gv) + 1e-08)

    remote(gos.at[2], gos.at[2], GO + 2, dev(y, z)).wait_recv()
    remote(gos.at[0], gos.at[0], GO + 0, dev(y, z)).wait_recv()
    remote(gos.at[1], gos.at[1], GO + 1, dev(y, z)).wait_recv()
    far_in = gos.at[3, pl.ds(0, 128)]
    remote(far_in, far_in, GO + 3, dev(y, z)).wait_recv()
    far_in = gos.at[3, pl.ds(128, 144)]
    remote(far_in, far_in, GO + 4, dev(y, z)).wait_recv()

    def gossip_gain(n):
        return gos[n, BLK:WROWS, 0:BLK].astype(F32)[0:1, :]

    mixed_g = share(0, BLK) * stepped_g
    mixed_g = mixed_g + share(3, BLK) * gossip_gain(0) + share(4, BLK) * gossip_gain(1)
    mixed_g = mixed_g + share(from_chip, BLK) * gossip_gain(2) + share(from_far, BLK) * gossip_gain(3)
    ng[0] = mixed_g

    col = jnp.sum(jnp.where(eye, jnp.broadcast_to(gain_row.astype(F32), (BLK, BLK)), 0.0), axis=1, keepdims=True)
    gcol[...] = jnp.broadcast_to(col, (BLK, 128))

    @pl.when(z == 0)
    def _():
        rr[z] = jnp.zeros((BLK, KV), BF16)

    @pl.when(z == 3)
    def _():
        rl[z] = jnp.zeros((BLK, KV), BF16)

    loads[3].wait()
    loads[4].wait()
    s0, s1, s2 = share(0, KV), share(3, KV), share(4, KV)
    s3, s4 = share(from_chip, KV), share(from_far, KV)

    def adam_rows(i, carry):
        rows = pl.ds(pl.multiple_of(i * 32, 32), 32)
        g = gbuf[z, rows, :] + rr[z, rows, :].astype(F32) + rl[z, rows, :].astype(F32)
        g = gcol[rows, 0:1] * g
        new_m = 0.9 * mv[rows, :] + 0.1 * g
        new_v = 0.999 * vv[rows, :] + 0.001 * g * g
        nm[rows, :] = new_m
        nv[rows, :] = new_v
        own = wf[rows, :]
        stepped = own - 0.01 * (new_m / (jnp.sqrt(new_v) + 1e-08) + 0.1 * own)
        out = s0 * stepped + s1 * gos[0, rows, :].astype(F32) + s2 * gos[1, rows, :].astype(F32)
        nw[rows, :] = out + s3 * gos[2, rows, :].astype(F32) + s4 * gos[3, rows, :].astype(F32)
        return carry

    def add_inner(i):
        for r in (1, 3, 2):
            ucopy(i, r).wait_recv()
        ats = [pl.multiple_of(yy * WIDE + unit_order(z, i) * BLK, BLK) for yy in range(4)]

        def rows_body(k, carry):
            rows = pl.ds(pl.multiple_of(k * 64, 64), 64)
            part = jnp.zeros((64, BLK), F32) if i == 0 else acc[rows, :]
            for yy in range(4):
                x = xv[rows, pl.ds(ats[yy], BLK)].astype(F32)
                part = part + ur[i][yy, rows, :].astype(F32) * x
            acc[rows, :] = part
            return carry

        lax.fori_loop(0, ROWS // 64, rows_body, 0)

    for h in (0, 1):
        add_inner(h)

        @pl.when(z > 0)
        def _():
            remote(rsend.at[z, half_rows(h)], rr.at[z, half_rows(h)], RR + 2 * z + h, dev(y, z)).wait_recv()

        @pl.when(z < 3)
        def _():
            remote(rsend.at[z, half_rows(h)], rl.at[z, half_rows(h)], RL + 2 * z + h, dev(y, z)).wait_recv()

        lax.fori_loop(4 * h, 4 * h + 4, adam_rows, 0)

    add_inner(2)
    add_inner(3)

    for _, copy in sent:
        copy.wait_send()
    for h in (0, 1):
        for s, right, left in (
            (0, z < 3, z > 0),
            (1, (z == 1) | (z == 2), (z == 1) | (z == 2)),
            (2, z == 2, z == 1),
        ):
            @pl.when(right)
            def _():
                wright(s, h).wait_send()

            @pl.when(left)
            def _():
                wleft(s, h).wait_send()

        for s in (2, 3):
            @pl.when(z == 3)
            def _():
                far(3 - s, h).wait_send()

            @pl.when(z == 0)
            def _():
                far(s, h).wait_send()

        for b in range(4):
            @pl.when(z < b)
            def _():
                rsright(b, h).wait_send()

            @pl.when(z > b)
            def _():
                rsleft(b, h).wait_send()


def finish_kernel(
    ur0, ur1, ur2, ur3, x, sc, acc, nw, nm, nv, ng, ngm, ngv,
    ig, nw_out, nm_out, nv_out, ng_out, ngm_out, ngv_out,
    grad, sem, grad_sem,
):
    writes = [
        pltpu.make_async_copy(nw, nw_out, sem.at[0]),
        pltpu.make_async_copy(nm, nm_out, sem.at[1]),
        pltpu.make_async_copy(nv, nv_out, sem.at[2]),
    ]
    for c in writes:
        c.start()
    ng_out[...] = ng[...]
    ngm_out[...] = ngm[...]
    ngv_out[...] = ngv[...]

    z = lax.axis_index("fsdp") % 4
    blocks = []
    for i, ref in enumerate((ur0, ur1, ur2, ur3)):
        for yy in range(4):
            at = pl.multiple_of(yy * WIDE + unit_order(z, i) * BLK, BLK)
            blocks.append((ref, yy, pl.ds(at, BLK)))

    def grad_rows(i, carry):
        rows = pl.ds(pl.multiple_of(i * 32, 32), 32)
        s = sc[rows, :]
        t = jnp.sum(acc[rows, :], axis=1, keepdims=True) * (1.0 / 4096)
        t = jnp.broadcast_to(t, (32, 128)) * (s * s * s)
        s, t = (jnp.concatenate([v, v], axis=1) for v in (s, t))
        for ref, yy, cols in blocks:
            grad[rows, cols] = s * ref[yy, rows, :].astype(F32) - x[rows, cols].astype(F32) * t
        return carry

    parts = grad_sem.shape[0]
    size = ROWS // parts
    for p in range(parts):
        lax.fori_loop(p * size // 32, (p + 1) * size // 32, grad_rows, 0)
        rows = pl.ds(p * size, size)
        c = pltpu.make_async_copy(grad.at[rows], ig.at[rows], grad_sem.at[p])
        c.start()
        writes.append(c)
    for c in writes:
        c.wait()


def body(inputs, value_grad, weight, weight_m, weight_v, gain, gain_m, gain_v, mixing):
    vmem = pl.BlockSpec(memory_space=pltpu.VMEM)
    hbm = pl.BlockSpec(memory_space=pl.ANY)
    tokens = inputs.reshape(ROWS, 4 * WIDE)
    shapes = [((ROWS, 4 * WIDE), F32)] + [((BLK, KV), F32)] * 3 + [((1, 1, BLK), F32)] * 3
    passed = [((4, ROWS, BLK), BF16)] * 4 + [((ROWS, 4 * WIDE), BF16), ((ROWS, 128), F32), ((ROWS, BLK), F32)]
    parts = pl.pallas_call(
        step_kernel,
        name="gossip_step",
        out_shape=[pltpu.VMEM(*a) for a in passed + shapes[1:]],
        in_specs=[pl.BlockSpec(memory_space=pltpu.SMEM)] + [hbm] * 5 + [vmem] * 3,
        out_specs=[vmem] * 13,
        scratch_shapes=[
            pltpu.VMEM((BLK, KV), F32),
            pltpu.VMEM((BLK, KV), F32),
            pltpu.VMEM((BLK, KV), F32),
            pltpu.VMEM((4 * ROWS, KV), BF16),
            pltpu.VMEM((4, 4, ROWS, BLK), BF16),
            pltpu.VMEM((4, 4 * ROWS, BLK), BF16),
            pltpu.VMEM((BLK, 4 * ROWS), BF16),
            pltpu.VMEM((4, WROWS, KV), BF16),
            pltpu.VMEM((4, 4 * ROWS, BLK), BF16),
            pltpu.VMEM((4, BLK, KV), F32),
            pltpu.VMEM((4, BLK, KV), BF16),
            pltpu.VMEM((4, BLK, KV), BF16),
            pltpu.VMEM((4, BLK, KV), BF16),
            pltpu.VMEM((4, 8, BLK), F32),
            pltpu.VMEM((3, 8, BLK), F32),
            pltpu.VMEM((4, WROWS, KV), BF16),
            pltpu.VMEM((BLK, 128), F32),
            pltpu.SemaphoreType.DMA((5,)),
            pltpu.SemaphoreType.DMA((NSEM,)),
            pltpu.SemaphoreType.DMA((NSEM,)),
        ],
        compiler_params=pltpu.CompilerParams(
            collective_id=0, has_side_effects=True, vmem_limit_bytes=50 << 20
        ),
    )(
        mixing,
        tokens,
        value_grad.reshape(ROWS, KV),
        weight[0, 0],
        weight_m[0, 0],
        weight_v[0, 0],
        gain,
        gain_m,
        gain_v,
    )
    ig, nw, nm, nv, ng, ngm, ngv = pl.pallas_call(
        finish_kernel,
        name="finish",
        out_shape=[jax.ShapeDtypeStruct(*a) for a in shapes],
        in_specs=[vmem] * 13,
        out_specs=[hbm] * 4 + [vmem] * 3,
        scratch_shapes=[
            pltpu.VMEM((ROWS, 4 * WIDE), F32),
            pltpu.SemaphoreType.DMA((3,)),
            pltpu.SemaphoreType.DMA((4,)),
        ],
        compiler_params=pltpu.CompilerParams(vmem_limit_bytes=16 << 20),
    )(*parts)
    return (ig.reshape(inputs.shape), nw[None, None], nm[None, None], nv[None, None], ng, ngm, ngv)


def solution(mesh):
    placed = (
        P("rx", "ry", None, "fsdp", None),
        P("rx", "ry", None, "fsdp", None),
        P("rx", "ry", "fsdp", None),
        P("rx", "ry", "fsdp", None),
        P("rx", "ry", "fsdp", None),
        P("rx", "ry", "fsdp"),
        P("rx", "ry", "fsdp"),
        P("rx", "ry", "fsdp"),
        P("rx", "ry", None),
    )
    return jax.shard_map(
        body,
        mesh=mesh,
        in_specs=placed,
        out_specs=(
            P("rx", "ry", None, "fsdp", None),
            P("rx", "ry", "fsdp", None),
            P("rx", "ry", "fsdp", None),
            P("rx", "ry", "fsdp", None),
            P("rx", "ry", "fsdp"),
            P("rx", "ry", "fsdp"),
            P("rx", "ry", "fsdp"),
        ),
        check_vma=False,
    )
```

```python
import jax
import jax.numpy as jnp
from jax import lax
from jax.experimental import pallas as pl
from jax.experimental.pallas import tpu as pltpu
from jax.sharding import PartitionSpec as P

MESH = pl.DeviceIdType.MESH
F32 = jnp.float32
BF16 = jnp.bfloat16

ROWS = 256
BLK = 256
KV = 1024
WIDE = 1024
WROWS = BLK + 16

VG = 0
WL = 12
WR = 28
NS = 44
US = 56
RR = 68
RL = 76
GG = 84
GO = 87
NSEM = 94


def KC(k):
    for lo, c in ((87, "GO"), (84, "GG"), (68, "RS"), (56, "US"), (44, "NS"), (12, "W"), (0, "VG")):
        if k >= lo:
            return c


def mirrored(z, codes, i):
    upper = z // 2
    near = z + upper * (3 - 2 * z)
    t = ((codes[0] + (codes[1] - codes[0]) * near) // 4**i) % 4
    return t + upper * (3 - 2 * t)


def grad_order(z, i):
    return mirrored(z, (27, 99), i)


def unit_order(z, i):
    return mirrored(z, (216, 225), i)


def step_kernel(
    mix, x_hbm, vg_hbm, w_hbm, m_hbm, v_hbm, gain, gain_m, gain_v,
    ur0, ur1, ur2, ur3, xv, sc, acc, nw, nm, nv, ng, ngm, ngv,
    wf, mv, vv, vgp, nown, npool, npt, wp, us, gbuf, rsend, rr, rl, gg, ggr, gos, gcol,
    lsem, ssem, rsem,
):
    ur = (ur0, ur1, ur2, ur3)
    rx = lax.axis_index("rx")
    ry = lax.axis_index("ry")
    f = lax.axis_index("fsdp")
    zh = rx // 2
    core = rx % 2
    y = f // 4
    z = f % 4

    def dev(yy, zz):
        return (rx, ry, yy * 4 + zz)

    def ypeer(r):
        return dev((y + r) % 4, z)

    far_rx = (1 - zh) * 2 + (1 - core)
    chip_rx = zh * 2 + (1 - core)

    def remote(src, dst, k, device):
        return pltpu.make_async_remote_copy(
            src_ref=src, dst_ref=dst, send_sem=ssem.at[k], recv_sem=rsem.at[k],
            device_id=device, device_id_type=MESH,
        )

    barrier = pltpu.get_barrier_semaphore()
    far_base = (1 - z // 2) * 2
    partners = [ypeer(1), ypeer(2), ypeer(3)]
    partners += [dev(y, (z + 1) % 4), dev(y, (z + 2) % 4), dev(y, (z + 3) % 4)]
    partners += [(rx, (ry + 1) % 4, f), (rx, (ry + 3) % 4, f), (chip_rx, ry, f)]
    partners += [(far_rx, ry, y * 4 + far_base), (far_rx, ry, y * 4 + far_base + 1)]
    for p in partners:
        pl.semaphore_signal(barrier, inc=1, device_id=p, device_id_type=MESH)
    loads = [
        pltpu.make_async_copy(w_hbm, wf, lsem.at[0]),
        pltpu.make_async_copy(x_hbm, xv, lsem.at[1]),
        pltpu.make_async_copy(vg_hbm, vgp.at[pl.ds(0, ROWS)], lsem.at[2]),
        pltpu.make_async_copy(m_hbm, mv, lsem.at[3]),
        pltpu.make_async_copy(v_hbm, vv, lsem.at[4]),
    ]
    for c in loads:
        c.start()

    loads[0].wait()
    gain_row = gain[0].astype(BF16)

    def cast_rows(i, carry):
        rows = pl.ds(pl.multiple_of(i * 32, 32), 32)
        wp[z, rows, :] = wf[rows, :].astype(BF16)
        return carry

    lax.fori_loop(0, BLK // 32, cast_rows, 0)
    wp[z, BLK:WROWS, :] = jnp.zeros((16, KV), BF16)
    wp[z, BLK:WROWS, 0:BLK] = jnp.broadcast_to(gain_row.astype(F32), (16, BLK)).astype(BF16)

    pl.semaphore_wait(barrier, len(partners))

    sent = []

    def go(copy, cond=None):
        copy.start()
        sent.append((cond, copy))

    def half(ref, slot, h, c):
        return ref.at[pl.ds(slot * ROWS + h * (ROWS // 2), ROWS // 2), pl.ds(c * (KV // 2), KV // 2)]

    def vg_own(c):
        for k, (r, h) in enumerate(((1, 0), (3, 1), (1, 1), (3, 0))):
            go(remote(half(vg_hbm, 0, h, c), half(vgp, r, h, c), VG + 6 * c + k, ypeer(r)))

    def vg_arrived(c, k, slot, h):
        remote(half(vgp, slot, h, c), half(vgp, slot, h, c), VG + 6 * c + k, ypeer(1)).wait_recv()

    def vg_relay(c):
        for k, (r, h) in enumerate(((1, 0), (3, 1))):
            vg_arrived(c, k, r, h)
            go(remote(half(vgp, r, h, c), half(vgp, 2, h, c), VG + 6 * c + 4 + k, ypeer(r)))

    def vg_all(c):
        for k, (r, h) in ((2, (1, 1)), (3, (3, 0)), (4, (2, 0)), (5, (2, 1))):
            vg_arrived(c, k, r, h)

    vg_own(0)

    def quarter(ref, block, q):
        return ref.at[block, pl.ds(q * 64, 64 + 16 * (q // 3))]

    def wright(s, q):
        return remote(quarter(wp, z - s, q), quarter(wp, z - s, q), WL + 4 * s + q, dev(y, z + 1))

    def wleft(s, q):
        return remote(quarter(wp, z + s, q), quarter(wp, z + s, q), WR + 4 * s + q, dev(y, z - 1))

    def from_left(s, q):
        remote(quarter(wp, z - s, q), quarter(wp, z - s, q), WL + 4 * s + q - 4, dev(y, z)).wait_recv()

    def from_right(s, q):
        remote(quarter(wp, z + s, q), quarter(wp, z + s, q), WR + 4 * s + q - 4, dev(y, z)).wait_recv()

    def far(zz, q):
        return remote(quarter(wp, zz, q), quarter(gos, 3, q), GO + 3 + q, (far_rx, ry, y * 4 + zz))

    @pl.when(z < 3)
    def _():
        wright(0, 0).start()

    @pl.when(z > 0)
    def _():
        wleft(0, 0).start()

    @pl.when(z < 2)
    def _():
        for q in (1, 2, 3):
            wright(0, q).start()

    @pl.when(z > 1)
    def _():
        for q in (1, 2, 3):
            wleft(0, q).start()

    go(remote(wp.at[z], gos.at[2], GO + 2, (chip_rx, ry, f)))
    go(remote(wp.at[z], gos.at[0], GO + 0, (rx, (ry + 1) % 4, f)))
    go(remote(wp.at[z], gos.at[1], GO + 1, (rx, (ry + 3) % 4, f)))

    vg_relay(0)
    vg_own(1)

    loads[1].wait()

    def norm_rows(i, carry):
        rows = pl.ds(pl.multiple_of(i * 64, 64), 64)
        part = jnp.zeros((64, 128), F32)
        for c in range(4 * WIDE // 128):
            x = xv[rows, c * 128:(c + 1) * 128].astype(F32)
            part = part + x * x
        s = lax.rsqrt(jnp.sum(part, axis=1, keepdims=True) * (1.0 / 4096) + 1e-05)
        s = jnp.broadcast_to(s, (64, 128))
        sc[rows, :] = s
        for yy in range(4):
            for b in range(4):
                for c in (0, 128):
                    at = yy * WIDE + b * BLK + c
                    nown[yy, b, rows, c:c + 128] = (xv[rows, at:at + 128].astype(F32) * s).astype(BF16)
        return carry

    lax.fori_loop(0, ROWS // 64, norm_rows, 0)

    def outwards(q):
        @pl.when(z == 2)
        def _():
            from_left(1, q)
            wright(1, q).start()

        @pl.when(z == 1)
        def _():
            from_right(1, q)
            wleft(1, q).start()

    outwards(0)

    def order(i):
        return grad_order(z, i)

    def slot(r):
        return pl.ds(r * ROWS, ROWS)

    def ncopy(i, r):
        b = order(i)
        return remote(nown.at[(y + r) % 4, b], npool.at[b, slot(r)], NS + 3 * i + r - 1, ypeer(r))

    for r in (1, 3, 2):
        go(ncopy(0, r))

    def own_rows(i, carry):
        rows = pl.ds(pl.multiple_of(i * 64, 64), 64)
        for b in range(4):
            npool[b, rows, :] = nown[y, b, rows, :]
        return carry

    lax.fori_loop(0, ROWS // 64, own_rows, 0)

    def part(ref, b, c):
        return ref.at[b, :, pl.ds(c * (KV // 2), KV // 2)]

    def rsright(b, c):
        return remote(part(rsend, b, c), part(rr, b, c), RR + 2 * b + c, dev(y, z + 1))

    def rsleft(b, c):
        return remote(part(rsend, b, c), part(rl, b, c), RL + 2 * b + c, dev(y, z - 1))

    def sums_in(b, c, ref, k):
        remote(part(rsend, b, c), part(ref, b, c), k + 2 * b + c, dev(y, z)).wait_recv()

    def round_half(b, c, other=None):
        cols = pl.ds(c * (KV // 2), KV // 2)

        def rows_body(i, carry):
            rows = pl.ds(pl.multiple_of(i * 32, 32), 32)
            g = gbuf[b, rows, cols]
            if other is not None:
                g = g + other[b, rows, cols].astype(F32)
            rsend[b, rows, cols] = g.astype(BF16)
            return carry

        lax.fori_loop(0, BLK // 32, rows_body, 0)

    def weight_grad(i, c):
        b = order(i)
        if c == 0:
            for r in (1, 3, 2):
                ncopy(i, r).wait_recv()
            npt[...] = npool[b].T

        def columns(k, carry):
            cols = pl.ds(pl.multiple_of(c * (KV // 2) + k * 256, 256), 256)
            gbuf[b, :, cols] = jnp.dot(npt[...], vgp[:, cols], preferred_element_type=F32)
            return carry

        lax.fori_loop(0, KV // 512, columns, 0)
        if i < 3:
            @pl.when(z == 0)
            def _():
                round_half(3 - i, c)
                rsright(3 - i, c).start()

            @pl.when(z == 3)
            def _():
                round_half(i, c)
                rsleft(i, c).start()

    def ucopy(i, r):
        b = unit_order(z, i)
        return remote(us.at[b, slot(r)], ur[i].at[y], US + 3 * i + r - 1, ypeer(4 - r))

    def unit_grad(i):
        b = unit_order(z, i)
        gl = wp[b, BLK:WROWS, 0:BLK].astype(F32)[0:1, :]

        def tokens(r, carry):
            rows = pl.ds(pl.multiple_of(r * ROWS, ROWS), ROWS)
            og = lax.dot_general(
                vgp[rows, :], wp[b, 0:BLK, :], (((1,), (1,)), ((), ())), preferred_element_type=F32
            )
            us[b, rows, :] = (og * gl).astype(BF16)
            return carry

        lax.fori_loop(0, 4, tokens, 0)
        for r in (1, 3, 2):
            go(ucopy(i, r))
        ur[i][y] = us[b, 0:ROWS, :]

    eye = lax.broadcasted_iota(jnp.int32, (BLK, BLK), 0) == lax.broadcasted_iota(jnp.int32, (BLK, BLK), 1)

    def gain_grad(b):
        def rows_body(i, carry):
            rows = pl.ds(pl.multiple_of(i * 64, 64), 64)
            part = jnp.zeros((64, 128), F32)
            for c in range(KV // 128):
                cols = pl.ds(c * 128, 128)
                part = part + wp[b, rows, cols].astype(F32) * gbuf[b, rows, cols]
            gcol[rows, :] = part
            return carry

        lax.fori_loop(0, BLK // 64, rows_body, 0)
        col = jnp.sum(gcol[...], axis=1, keepdims=True)
        spread = jnp.where(eye, jnp.broadcast_to(col, (BLK, BLK)), 0.0)
        gg[b] = jnp.sum(spread.reshape(BLK // 8, 8, BLK), axis=0)

    def relay_right(s):
        for q in range(4):
            from_left(s, q)
            wright(s, q).start()

    def relay_left(s):
        for q in range(4):
            from_right(s, q)
            wleft(s, q).start()

    def gossip_out(s, q):
        @pl.when(z == 3)
        def _():
            from_left(s, q)
            far(3 - s, q).start()

        @pl.when(z == 0)
        def _():
            from_right(s, q)
            far(s, q).start()

    def forward_right(b, c):
        sums_in(b, c, rr, RR)
        round_half(b, c, rr)
        rsright(b, c).start()

    def forward_left(b, c):
        sums_in(b, c, rl, RL)
        round_half(b, c, rl)
        rsleft(b, c).start()

    def forward_first(h):
        @pl.when(z == 1)
        def _():
            forward_right(3, h)

        @pl.when(z == 2)
        def _():
            forward_left(0, h)

    def forward_second(h):
        @pl.when(z == 1)
        def _():
            forward_left(0, h)
            forward_right(2, h)

        @pl.when(z == 2)
        def _():
            forward_right(3, h)
            forward_left(1, h)

    outwards(1)
    gossip_out(2, 0)
    vg_relay(1)
    for i in (1, 2, 3):
        for r in (1, 3, 2):
            go(ncopy(i, r))
    outwards(2)
    gossip_out(2, 1)
    outwards(3)
    gossip_out(2, 2)

    @pl.when(z == 2)
    def _():
        for q in (1, 2, 3):
            wright(0, q).start()
        relay_left(1)

    @pl.when(z == 1)
    def _():
        for q in (1, 2, 3):
            wleft(0, q).start()
        relay_right(1)

    loads[2].wait()
    gossip_out(2, 3)
    vg_all(0)
    weight_grad(0, 0)
    vg_all(1)
    weight_grad(0, 1)
    unit_grad(0)

    @pl.when(z == 2)
    def _():
        relay_right(2)

    @pl.when(z == 1)
    def _():
        relay_left(2)

    unit_grad(1)
    weight_grad(1, 0)
    weight_grad(1, 1)
    forward_first(0)

    @pl.when(z == 3)
    def _():
        for q in range(4):
            from_left(1, q)

    @pl.when(z == 0)
    def _():
        for q in range(4):
            from_right(1, q)

    unit_grad(2)
    weight_grad(2, 0)
    weight_grad(2, 1)
    for q in range(4):
        gossip_out(3, q)
    forward_first(1)
    unit_grad(3)
    weight_grad(3, 0)
    weight_grad(3, 1)
    forward_second(0)

    def gain_block(b, carry):
        gain_grad(b)
        return carry

    lax.fori_loop(0, 4, gain_block, 0)

    def ggcopy(d):
        zz = (z + d) % 4
        return remote(gg.at[zz], ggr.at[d - 1], GG + d - 1, dev(y, zz))

    for d in (1, 2, 3):
        go(ggcopy(d))

    forward_second(1)

    total = (mix[0, 0, 0] + mix[0, 0, 1] + mix[0, 0, 2] + mix[0, 0, 3] + mix[0, 0, 4]).astype(F32)

    def share(n, width):
        return jnp.full((1, width), mix[0, 0, n].astype(F32), F32) / jnp.full((1, width), total, F32)

    from_chip, from_far = 2 - core, 1 + core

    for d in (1, 2, 3):
        ggcopy(d).wait_recv()
    g8 = gg[z] + ggr[0] + ggr[1] + ggr[2]
    grad_gain = jnp.sum(g8, axis=0, keepdims=True)
    own_gain = gain[0]
    new_gm = 0.9 * gain_m[0] + 0.1 * grad_gain
    new_gv = 0.999 * gain_v[0] + 0.001 * grad_gain * grad_gain
    ngm[0] = new_gm
    ngv[0] = new_gv
    stepped_g = own_gain - 0.01 * new_gm / (jnp.sqrt(new_gv) + 1e-08)

    remote(gos.at[2], gos.at[2], GO + 2, dev(y, z)).wait_recv()
    remote(gos.at[0], gos.at[0], GO + 0, dev(y, z)).wait_recv()
    remote(gos.at[1], gos.at[1], GO + 1, dev(y, z)).wait_recv()
    for q in range(4):
        far_in = quarter(gos, 3, q)
        remote(far_in, far_in, GO + 3 + q, dev(y, z)).wait_recv()

    def gossip_gain(n):
        return gos[n, BLK:WROWS, 0:BLK].astype(F32)[0:1, :]

    mixed_g = share(0, BLK) * stepped_g
    mixed_g = mixed_g + share(3, BLK) * gossip_gain(0) + share(4, BLK) * gossip_gain(1)
    mixed_g = mixed_g + share(from_chip, BLK) * gossip_gain(2) + share(from_far, BLK) * gossip_gain(3)
    ng[0] = mixed_g

    col = jnp.sum(jnp.where(eye, jnp.broadcast_to(gain_row.astype(F32), (BLK, BLK)), 0.0), axis=1, keepdims=True)
    gcol[...] = jnp.broadcast_to(col, (BLK, 128))

    @pl.when(z == 0)
    def _():
        rr[z] = jnp.zeros((BLK, KV), BF16)

    @pl.when(z == 3)
    def _():
        rl[z] = jnp.zeros((BLK, KV), BF16)

    loads[3].wait()
    loads[4].wait()
    s0, s1, s2 = share(0, KV // 2), share(3, KV // 2), share(4, KV // 2)
    s3, s4 = share(from_chip, KV // 2), share(from_far, KV // 2)

    for c in (0, 1):
        cols = pl.ds(c * (KV // 2), KV // 2)

        def mix_rows(i, carry):
            rows = pl.ds(pl.multiple_of(i * 32, 32), 32)
            own = wf[rows, cols]
            out = s0 * (own - 0.01 * (0.1 * own))
            out = out + s1 * gos[0, rows, cols].astype(F32) + s2 * gos[1, rows, cols].astype(F32)
            nw[rows, cols] = out + s3 * gos[2, rows, cols].astype(F32) + s4 * gos[3, rows, cols].astype(F32)
            return carry

        lax.fori_loop(0, BLK // 32, mix_rows, 0)

    def adam(c):
        cols = pl.ds(c * (KV // 2), KV // 2)

        def adam_rows(i, carry):
            rows = pl.ds(pl.multiple_of(i * 32, 32), 32)
            g = gbuf[z, rows, cols] + rr[z, rows, cols].astype(F32) + rl[z, rows, cols].astype(F32)
            g = gcol[rows, 0:1] * g
            new_m = 0.9 * mv[rows, cols] + 0.1 * g
            new_v = 0.999 * vv[rows, cols] + 0.001 * g * g
            nm[rows, cols] = new_m
            nv[rows, cols] = new_v
            nw[rows, cols] = nw[rows, cols] - s0 * (0.01 * (new_m / (jnp.sqrt(new_v) + 1e-08)))
            return carry

        lax.fori_loop(0, BLK // 32, adam_rows, 0)

    def add_inner(i):
        for r in (1, 3, 2):
            ucopy(i, r).wait_recv()
        ats = [pl.multiple_of(yy * WIDE + unit_order(z, i) * BLK, BLK) for yy in range(4)]

        def rows_body(k, carry):
            rows = pl.ds(pl.multiple_of(k * 64, 64), 64)
            part = jnp.zeros((64, BLK), F32) if i == 0 else acc[rows, :]
            for yy in range(4):
                x = xv[rows, pl.ds(ats[yy], BLK)].astype(F32)
                part = part + ur[i][yy, rows, :].astype(F32) * x
            acc[rows, :] = part
            return carry

        lax.fori_loop(0, ROWS // 64, rows_body, 0)

    for c in (0, 1):
        add_inner(c)

        @pl.when(z > 0)
        def _():
            sums_in(z, c, rr, RR)

        @pl.when(z < 3)
        def _():
            sums_in(z, c, rl, RL)

        adam(c)

    add_inner(2)
    add_inner(3)

    for _, copy in sent:
        copy.wait_send()
    for q in range(4):
        for s, right, left in (
            (0, z < 3, z > 0),
            (1, (z == 1) | (z == 2), (z == 1) | (z == 2)),
            (2, z == 2, z == 1),
        ):
            @pl.when(right)
            def _():
                wright(s, q).wait_send()

            @pl.when(left)
            def _():
                wleft(s, q).wait_send()

        for s in (2, 3):
            @pl.when(z == 3)
            def _():
                far(3 - s, q).wait_send()

            @pl.when(z == 0)
            def _():
                far(s, q).wait_send()

    for h in (0, 1):
        for b in range(4):
            @pl.when(z < b)
            def _():
                rsright(b, h).wait_send()

            @pl.when(z > b)
            def _():
                rsleft(b, h).wait_send()


def finish_kernel(
    ur0, ur1, ur2, ur3, x, sc, acc, nw, nm, nv, ng, ngm, ngv,
    ig, nw_out, nm_out, nv_out, ng_out, ngm_out, ngv_out,
    grad, sem, grad_sem,
):
    writes = [
        pltpu.make_async_copy(nw, nw_out, sem.at[0]),
        pltpu.make_async_copy(nm, nm_out, sem.at[1]),
        pltpu.make_async_copy(nv, nv_out, sem.at[2]),
    ]
    for c in writes:
        c.start()
    ng_out[...] = ng[...]
    ngm_out[...] = ngm[...]
    ngv_out[...] = ngv[...]

    z = lax.axis_index("fsdp") % 4
    blocks = []
    for i, ref in enumerate((ur0, ur1, ur2, ur3)):
        for yy in range(4):
            at = pl.multiple_of(yy * WIDE + unit_order(z, i) * BLK, BLK)
            blocks.append((ref, yy, pl.ds(at, BLK)))

    def grad_rows(i, carry):
        rows = pl.ds(pl.multiple_of(i * 32, 32), 32)
        s = sc[rows, :]
        t = jnp.sum(acc[rows, :], axis=1, keepdims=True) * (1.0 / 4096)
        t = jnp.broadcast_to(t, (32, 128)) * (s * s * s)
        s, t = (jnp.concatenate([v, v], axis=1) for v in (s, t))
        for ref, yy, cols in blocks:
            grad[rows, cols] = s * ref[yy, rows, :].astype(F32) - x[rows, cols].astype(F32) * t
        return carry

    parts = grad_sem.shape[0]
    size = ROWS // parts
    for p in range(parts):
        lax.fori_loop(p * size // 32, (p + 1) * size // 32, grad_rows, 0)
        rows = pl.ds(p * size, size)
        c = pltpu.make_async_copy(grad.at[rows], ig.at[rows], grad_sem.at[p])
        c.start()
        writes.append(c)
    for c in writes:
        c.wait()


def body(inputs, value_grad, weight, weight_m, weight_v, gain, gain_m, gain_v, mixing):
    vmem = pl.BlockSpec(memory_space=pltpu.VMEM)
    hbm = pl.BlockSpec(memory_space=pl.ANY)
    tokens = inputs.reshape(ROWS, 4 * WIDE)
    shapes = [((ROWS, 4 * WIDE), F32)] + [((BLK, KV), F32)] * 3 + [((1, 1, BLK), F32)] * 3
    passed = [((4, ROWS, BLK), BF16)] * 4 + [((ROWS, 4 * WIDE), BF16), ((ROWS, 128), F32), ((ROWS, BLK), F32)]
    parts = pl.pallas_call(
        step_kernel,
        name="gossip_step",
        out_shape=[pltpu.VMEM(*a) for a in passed + shapes[1:]],
        in_specs=[pl.BlockSpec(memory_space=pltpu.SMEM)] + [hbm] * 5 + [vmem] * 3,
        out_specs=[vmem] * 13,
        scratch_shapes=[
            pltpu.VMEM((BLK, KV), F32),
            pltpu.VMEM((BLK, KV), F32),
            pltpu.VMEM((BLK, KV), F32),
            pltpu.VMEM((4 * ROWS, KV), BF16),
            pltpu.VMEM((4, 4, ROWS, BLK), BF16),
            pltpu.VMEM((4, 4 * ROWS, BLK), BF16),
            pltpu.VMEM((BLK, 4 * ROWS), BF16),
            pltpu.VMEM((4, WROWS, KV), BF16),
            pltpu.VMEM((4, 4 * ROWS, BLK), BF16),
            pltpu.VMEM((4, BLK, KV), F32),
            pltpu.VMEM((4, BLK, KV), BF16),
            pltpu.VMEM((4, BLK, KV), BF16),
            pltpu.VMEM((4, BLK, KV), BF16),
            pltpu.VMEM((4, 8, BLK), F32),
            pltpu.VMEM((3, 8, BLK), F32),
            pltpu.VMEM((4, WROWS, KV), BF16),
            pltpu.VMEM((BLK, 128), F32),
            pltpu.SemaphoreType.DMA((5,)),
            pltpu.SemaphoreType.DMA((NSEM,)),
            pltpu.SemaphoreType.DMA((NSEM,)),
        ],
        compiler_params=pltpu.CompilerParams(
            collective_id=0, has_side_effects=True, vmem_limit_bytes=50 << 20
        ),
    )(
        mixing,
        tokens,
        value_grad.reshape(ROWS, KV),
        weight[0, 0],
        weight_m[0, 0],
        weight_v[0, 0],
        gain,
        gain_m,
        gain_v,
    )
    ig, nw, nm, nv, ng, ngm, ngv = pl.pallas_call(
        finish_kernel,
        name="finish",
        out_shape=[jax.ShapeDtypeStruct(*a) for a in shapes],
        in_specs=[vmem] * 13,
        out_specs=[hbm] * 4 + [vmem] * 3,
        scratch_shapes=[
            pltpu.VMEM((ROWS, 4 * WIDE), F32),
            pltpu.SemaphoreType.DMA((3,)),
            pltpu.SemaphoreType.DMA((4,)),
        ],
        compiler_params=pltpu.CompilerParams(vmem_limit_bytes=16 << 20),
    )(*parts)
    return (ig.reshape(inputs.shape), nw[None, None], nm[None, None], nv[None, None], ng, ngm, ngv)


def solution(mesh):
    placed = (
        P("rx", "ry", None, "fsdp", None),
        P("rx", "ry", None, "fsdp", None),
        P("rx", "ry", "fsdp", None),
        P("rx", "ry", "fsdp", None),
        P("rx", "ry", "fsdp", None),
        P("rx", "ry", "fsdp"),
        P("rx", "ry", "fsdp"),
        P("rx", "ry", "fsdp"),
        P("rx", "ry", None),
    )
    return jax.shard_map(
        body,
        mesh=mesh,
        in_specs=placed,
        out_specs=(
            P("rx", "ry", None, "fsdp", None),
            P("rx", "ry", "fsdp", None),
            P("rx", "ry", "fsdp", None),
            P("rx", "ry", "fsdp", None),
            P("rx", "ry", "fsdp"),
            P("rx", "ry", "fsdp"),
            P("rx", "ry", "fsdp"),
        ),
        check_vma=False,
    )
```

```python
import jax
import jax.numpy as jnp
from jax import lax
from jax.experimental import pallas as pl
from jax.experimental.pallas import tpu as pltpu
from jax.sharding import PartitionSpec as P

MESH = pl.DeviceIdType.MESH
F32 = jnp.float32
BF16 = jnp.bfloat16

ROWS = 256
BLK = 256
KV = 1024
WIDE = 1024
WROWS = BLK + 16

VG = 0
WL = 12
WR = 28
NS = 44
US = 56
RR = 68
RL = 76
GG = 84
GO = 87
NSEM = 94


def KC(k):
    for lo, c in ((87, "GO"), (84, "GG"), (68, "RS"), (56, "US"), (44, "NS"), (12, "W"), (0, "VG")):
        if k >= lo:
            return c


def mirrored(z, codes, i):
    upper = z // 2
    near = z + upper * (3 - 2 * z)
    t = ((codes[0] + (codes[1] - codes[0]) * near) // 4**i) % 4
    return t + upper * (3 - 2 * t)


def grad_order(z, i):
    return mirrored(z, (27, 99), i)


def unit_order(z, i):
    return mirrored(z, (216, 225), i)


def step_kernel(
    mix, x_hbm, vg_hbm, w_hbm, m_hbm, v_hbm, gain, gain_m, gain_v,
    ur0, ur1, ur2, ur3, xv, sc, acc, nw, nm, nv, ng, ngm, ngv,
    wf, mv, vv, vgp, nown, npool, npt, wp, us, gbuf, rsend, rr, rl, gg, ggr, gos, gcol,
    lsem, ssem, rsem,
):
    ur = (ur0, ur1, ur2, ur3)
    rx = lax.axis_index("rx")
    ry = lax.axis_index("ry")
    f = lax.axis_index("fsdp")
    zh = rx // 2
    core = rx % 2
    y = f // 4
    z = f % 4

    def dev(yy, zz):
        return (rx, ry, yy * 4 + zz)

    def ypeer(r):
        return dev((y + r) % 4, z)

    far_rx = (1 - zh) * 2 + (1 - core)
    chip_rx = zh * 2 + (1 - core)

    def remote(src, dst, k, device):
        return pltpu.make_async_remote_copy(
            src_ref=src, dst_ref=dst, send_sem=ssem.at[k], recv_sem=rsem.at[k],
            device_id=device, device_id_type=MESH,
        )

    barrier = pltpu.get_barrier_semaphore()
    far_base = (1 - z // 2) * 2
    partners = [ypeer(1), ypeer(2), ypeer(3)]
    partners += [dev(y, (z + 1) % 4), dev(y, (z + 2) % 4), dev(y, (z + 3) % 4)]
    partners += [(rx, (ry + 1) % 4, f), (rx, (ry + 3) % 4, f), (chip_rx, ry, f)]
    partners += [(far_rx, ry, y * 4 + far_base), (far_rx, ry, y * 4 + far_base + 1)]
    for p in partners:
        pl.semaphore_signal(barrier, inc=1, device_id=p, device_id_type=MESH)
    loads = [
        pltpu.make_async_copy(w_hbm, wf, lsem.at[0]),
        pltpu.make_async_copy(x_hbm, xv, lsem.at[1]),
        pltpu.make_async_copy(vg_hbm, vgp.at[pl.ds(0, ROWS)], lsem.at[2]),
        pltpu.make_async_copy(m_hbm, mv, lsem.at[3]),
        pltpu.make_async_copy(v_hbm, vv, lsem.at[4]),
    ]
    for k in (0, 1):
        loads[k].start()

    pl.semaphore_wait(barrier, len(partners))

    sent, sent_units = [], []

    def go(copy, to=sent):
        copy.start()
        to.append(copy)

    def half(ref, slot, h, c):
        return ref.at[pl.ds(slot * ROWS + h * (ROWS // 2), ROWS // 2), pl.ds(c * (KV // 2), KV // 2)]

    def vg_own(c):
        for k, (r, h) in enumerate(((1, 0), (3, 1), (1, 1), (3, 0))):
            go(remote(half(vg_hbm, 0, h, c), half(vgp, r, h, c), VG + 6 * c + k, ypeer(r)))

    def vg_arrived(c, k, slot, h):
        remote(half(vgp, slot, h, c), half(vgp, slot, h, c), VG + 6 * c + k, ypeer(1)).wait_recv()

    def vg_relay(c):
        for k, (r, h) in enumerate(((1, 0), (3, 1))):
            vg_arrived(c, k, r, h)
            go(remote(half(vgp, r, h, c), half(vgp, 2, h, c), VG + 6 * c + 4 + k, ypeer(r)))

    def vg_all(c):
        for k, (r, h) in ((2, (1, 1)), (3, (3, 0)), (4, (2, 0)), (5, (2, 1))):
            vg_arrived(c, k, r, h)

    vg_own(0)
    for k in (2, 3, 4):
        loads[k].start()

    loads[0].wait()
    gain_row = gain[0].astype(BF16)

    def cast_rows(i, carry):
        rows = pl.ds(pl.multiple_of(i * 32, 32), 32)
        wp[z, rows, :] = wf[rows, :].astype(BF16)
        return carry

    lax.fori_loop(0, BLK // 32, cast_rows, 0)
    wp[z, BLK:WROWS, :] = jnp.zeros((16, KV), BF16)
    wp[z, BLK:WROWS, 0:BLK] = jnp.broadcast_to(gain_row.astype(F32), (16, BLK)).astype(BF16)


    def quarter(ref, block, q):
        return ref.at[block, pl.ds(q * 64, 64 + 16 * (q // 3))]

    def wright(s, q):
        return remote(quarter(wp, z - s, q), quarter(wp, z - s, q), WL + 4 * s + q, dev(y, z + 1))

    def wleft(s, q):
        return remote(quarter(wp, z + s, q), quarter(wp, z + s, q), WR + 4 * s + q, dev(y, z - 1))

    def from_left(s, q):
        remote(quarter(wp, z - s, q), quarter(wp, z - s, q), WL + 4 * s + q - 4, dev(y, z)).wait_recv()

    def from_right(s, q):
        remote(quarter(wp, z + s, q), quarter(wp, z + s, q), WR + 4 * s + q - 4, dev(y, z)).wait_recv()

    def far(zz, q):
        return remote(quarter(wp, zz, q), quarter(gos, 3, q), GO + 3 + q, (far_rx, ry, y * 4 + zz))

    @pl.when(z < 3)
    def _():
        wright(0, 0).start()

    @pl.when(z > 0)
    def _():
        wleft(0, 0).start()

    @pl.when(z < 2)
    def _():
        for q in (1, 2, 3):
            wright(0, q).start()

    @pl.when(z > 1)
    def _():
        for q in (1, 2, 3):
            wleft(0, q).start()

    go(remote(wp.at[z], gos.at[2], GO + 2, (chip_rx, ry, f)))
    go(remote(wp.at[z], gos.at[0], GO + 0, (rx, (ry + 1) % 4, f)))
    go(remote(wp.at[z], gos.at[1], GO + 1, (rx, (ry + 3) % 4, f)))

    vg_relay(0)
    vg_own(1)

    loads[1].wait()

    def norm_rows(i, carry):
        rows = pl.ds(pl.multiple_of(i * 64, 64), 64)
        part = jnp.zeros((64, 128), F32)
        for c in range(4 * WIDE // 128):
            x = xv[rows, c * 128:(c + 1) * 128].astype(F32)
            part = part + x * x
        s = lax.rsqrt(jnp.sum(part, axis=1, keepdims=True) * (1.0 / 4096) + 1e-05)
        s = jnp.broadcast_to(s, (64, 128))
        sc[rows, :] = s
        for yy in range(4):
            for b in range(4):
                for c in (0, 128):
                    at = yy * WIDE + b * BLK + c
                    nown[yy, b, rows, c:c + 128] = (xv[rows, at:at + 128].astype(F32) * s).astype(BF16)
        return carry

    lax.fori_loop(0, ROWS // 64, norm_rows, 0)

    def outwards(q):
        @pl.when(z == 2)
        def _():
            from_left(1, q)
            wright(1, q).start()

        @pl.when(z == 1)
        def _():
            from_right(1, q)
            wleft(1, q).start()

    outwards(0)

    def order(i):
        return grad_order(z, i)

    def slot(r):
        return pl.ds(r * ROWS, ROWS)

    def ncopy(i, r):
        b = order(i)
        return remote(nown.at[(y + r) % 4, b], npool.at[b, slot(r)], NS + 3 * i + r - 1, ypeer(r))

    for r in (1, 3, 2):
        go(ncopy(0, r))

    def own_rows(i, carry):
        rows = pl.ds(pl.multiple_of(i * 64, 64), 64)
        for b in range(4):
            npool[b, rows, :] = nown[y, b, rows, :]
        return carry

    lax.fori_loop(0, ROWS // 64, own_rows, 0)

    def part(ref, b, c):
        return ref.at[b, :, pl.ds(c * (KV // 2), KV // 2)]

    def rsright(b, c):
        return remote(part(rsend, b, c), part(rr, b, c), RR + 2 * b + c, dev(y, z + 1))

    def rsleft(b, c):
        return remote(part(rsend, b, c), part(rl, b, c), RL + 2 * b + c, dev(y, z - 1))

    def sums_in(b, c, ref, k):
        remote(part(rsend, b, c), part(ref, b, c), k + 2 * b + c, dev(y, z)).wait_recv()

    def round_half(b, c, other=None):
        cols = pl.ds(c * (KV // 2), KV // 2)

        def rows_body(i, carry):
            rows = pl.ds(pl.multiple_of(i * 32, 32), 32)
            g = gbuf[b, rows, cols]
            if other is not None:
                g = g + other[b, rows, cols].astype(F32)
            rsend[b, rows, cols] = g.astype(BF16)
            return carry

        lax.fori_loop(0, BLK // 32, rows_body, 0)

    def weight_grad(i, c):
        b = order(i)
        if c == 0:
            for r in (1, 3, 2):
                ncopy(i, r).wait_recv()
            npt[...] = npool[b].T

        def columns(k, carry):
            cols = pl.ds(pl.multiple_of(c * (KV // 2) + k * 256, 256), 256)
            gbuf[b, :, cols] = jnp.dot(npt[...], vgp[:, cols], preferred_element_type=F32)
            return carry

        lax.fori_loop(0, KV // 512, columns, 0)
        if i < 3:
            @pl.when(z == 0)
            def _():
                round_half(3 - i, c)
                rsright(3 - i, c).start()

            @pl.when(z == 3)
            def _():
                round_half(i, c)
                rsleft(i, c).start()

    def ucopy(i, r):
        b = unit_order(z, i)
        return remote(us.at[b, slot(r)], ur[i].at[y], US + 3 * i + r - 1, ypeer(4 - r))

    def unit_grad(i):
        b = unit_order(z, i)
        gl = wp[b, BLK:WROWS, 0:BLK].astype(F32)[0:1, :]

        def tokens(r, carry):
            rows = pl.ds(pl.multiple_of(r * ROWS, ROWS), ROWS)
            og = lax.dot_general(
                vgp[rows, :], wp[b, 0:BLK, :], (((1,), (1,)), ((), ())), preferred_element_type=F32
            )
            us[b, rows, :] = (og * gl).astype(BF16)
            return carry

        lax.fori_loop(0, 4, tokens, 0)
        for r in (2, 1, 3):
            go(ucopy(i, r), sent_units)
        ur[i][y] = us[b, 0:ROWS, :]

    eye = lax.broadcasted_iota(jnp.int32, (BLK, BLK), 0) == lax.broadcasted_iota(jnp.int32, (BLK, BLK), 1)

    def gain_grad(b):
        def rows_body(i, carry):
            rows = pl.ds(pl.multiple_of(i * 64, 64), 64)
            part = jnp.zeros((64, 128), F32)
            for c in range(KV // 128):
                cols = pl.ds(c * 128, 128)
                part = part + wp[b, rows, cols].astype(F32) * gbuf[b, rows, cols]
            gcol[rows, :] = part
            return carry

        lax.fori_loop(0, BLK // 64, rows_body, 0)
        col = jnp.sum(gcol[...], axis=1, keepdims=True)
        spread = jnp.where(eye, jnp.broadcast_to(col, (BLK, BLK)), 0.0)
        gg[b] = jnp.sum(spread.reshape(BLK // 8, 8, BLK), axis=0)

    def relay_right(s):
        for q in range(4):
            from_left(s, q)
            wright(s, q).start()

    def relay_left(s):
        for q in range(4):
            from_right(s, q)
            wleft(s, q).start()

    def gossip_out(s, q):
        @pl.when(z == 3)
        def _():
            from_left(s, q)
            far(3 - s, q).start()

        @pl.when(z == 0)
        def _():
            from_right(s, q)
            far(s, q).start()

    def forward_right(b, c):
        sums_in(b, c, rr, RR)
        round_half(b, c, rr)
        rsright(b, c).start()

    def forward_left(b, c):
        sums_in(b, c, rl, RL)
        round_half(b, c, rl)
        rsleft(b, c).start()

    def forward_first(h):
        @pl.when(z == 1)
        def _():
            forward_right(3, h)

        @pl.when(z == 2)
        def _():
            forward_left(0, h)

    def forward_second(h):
        @pl.when(z == 1)
        def _():
            forward_left(0, h)
            forward_right(2, h)

        @pl.when(z == 2)
        def _():
            forward_right(3, h)
            forward_left(1, h)

    outwards(1)
    gossip_out(2, 0)
    vg_relay(1)
    for i in (1, 2, 3):
        for r in (1, 3, 2):
            go(ncopy(i, r))
    outwards(2)
    gossip_out(2, 1)
    outwards(3)
    gossip_out(2, 2)

    @pl.when(z == 2)
    def _():
        for q in (1, 2, 3):
            wright(0, q).start()
        relay_left(1)

    @pl.when(z == 1)
    def _():
        for q in (1, 2, 3):
            wleft(0, q).start()
        relay_right(1)

    loads[2].wait()
    gossip_out(2, 3)
    vg_all(0)
    weight_grad(0, 0)
    vg_all(1)
    weight_grad(0, 1)
    unit_grad(0)

    @pl.when(z == 2)
    def _():
        relay_right(2)

    @pl.when(z == 1)
    def _():
        relay_left(2)

    unit_grad(1)
    weight_grad(1, 0)
    weight_grad(1, 1)
    forward_first(0)

    @pl.when(z == 3)
    def _():
        for q in range(4):
            from_left(1, q)

    @pl.when(z == 0)
    def _():
        for q in range(4):
            from_right(1, q)

    unit_grad(2)
    weight_grad(2, 0)
    weight_grad(2, 1)
    for q in range(4):
        gossip_out(3, q)
    forward_first(1)
    unit_grad(3)
    weight_grad(3, 0)
    weight_grad(3, 1)
    forward_second(0)

    def gain_block(b, carry):
        gain_grad(b)
        return carry

    lax.fori_loop(0, 4, gain_block, 0)

    def ggcopy(d):
        zz = (z + d) % 4
        return remote(gg.at[zz], ggr.at[d - 1], GG + d - 1, dev(y, zz))

    for d in (1, 2, 3):
        go(ggcopy(d))

    forward_second(1)

    total = (mix[0, 0, 0] + mix[0, 0, 1] + mix[0, 0, 2] + mix[0, 0, 3] + mix[0, 0, 4]).astype(F32)

    def share(n, width):
        return jnp.full((1, width), mix[0, 0, n].astype(F32), F32) / jnp.full((1, width), total, F32)

    from_chip, from_far = 2 - core, 1 + core

    for d in (1, 2, 3):
        ggcopy(d).wait_recv()
    g8 = gg[z] + ggr[0] + ggr[1] + ggr[2]
    grad_gain = jnp.sum(g8, axis=0, keepdims=True)
    own_gain = gain[0]
    new_gm = 0.9 * gain_m[0] + 0.1 * grad_gain
    new_gv = 0.999 * gain_v[0] + 0.001 * grad_gain * grad_gain
    ngm[0] = new_gm
    ngv[0] = new_gv
    stepped_g = own_gain - 0.01 * new_gm / (jnp.sqrt(new_gv) + 1e-08)

    remote(gos.at[2], gos.at[2], GO + 2, dev(y, z)).wait_recv()
    remote(gos.at[0], gos.at[0], GO + 0, dev(y, z)).wait_recv()
    remote(gos.at[1], gos.at[1], GO + 1, dev(y, z)).wait_recv()
    for q in range(4):
        far_in = quarter(gos, 3, q)
        remote(far_in, far_in, GO + 3 + q, dev(y, z)).wait_recv()

    def gossip_gain(n):
        return gos[n, BLK:WROWS, 0:BLK].astype(F32)[0:1, :]

    mixed_g = share(0, BLK) * stepped_g
    mixed_g = mixed_g + share(3, BLK) * gossip_gain(0) + share(4, BLK) * gossip_gain(1)
    mixed_g = mixed_g + share(from_chip, BLK) * gossip_gain(2) + share(from_far, BLK) * gossip_gain(3)
    ng[0] = mixed_g

    col = jnp.sum(jnp.where(eye, jnp.broadcast_to(gain_row.astype(F32), (BLK, BLK)), 0.0), axis=1, keepdims=True)
    gcol[...] = jnp.broadcast_to(col, (BLK, 128))

    @pl.when(z == 0)
    def _():
        rr[z] = jnp.zeros((BLK, KV), BF16)

    @pl.when(z == 3)
    def _():
        rl[z] = jnp.zeros((BLK, KV), BF16)

    loads[3].wait()
    loads[4].wait()
    s0, s1, s2 = share(0, KV // 2), share(3, KV // 2), share(4, KV // 2)
    s3, s4 = share(from_chip, KV // 2), share(from_far, KV // 2)

    for c in (0, 1):
        cols = pl.ds(c * (KV // 2), KV // 2)

        def mix_rows(i, carry):
            rows = pl.ds(pl.multiple_of(i * 32, 32), 32)
            own = wf[rows, cols]
            out = s0 * (own - 0.01 * (0.1 * own))
            out = out + s1 * gos[0, rows, cols].astype(F32) + s2 * gos[1, rows, cols].astype(F32)
            nw[rows, cols] = out + s3 * gos[2, rows, cols].astype(F32) + s4 * gos[3, rows, cols].astype(F32)
            return carry

        lax.fori_loop(0, BLK // 32, mix_rows, 0)

    def adam(c):
        cols = pl.ds(c * (KV // 2), KV // 2)

        def adam_rows(i, carry):
            rows = pl.ds(pl.multiple_of(i * 32, 32), 32)
            g = gbuf[z, rows, cols] + rr[z, rows, cols].astype(F32) + rl[z, rows, cols].astype(F32)
            g = gcol[rows, 0:1] * g
            new_m = 0.9 * mv[rows, cols] + 0.1 * g
            new_v = 0.999 * vv[rows, cols] + 0.001 * g * g
            nm[rows, cols] = new_m
            nv[rows, cols] = new_v
            nw[rows, cols] = nw[rows, cols] - s0 * (0.01 * (new_m / (jnp.sqrt(new_v) + 1e-08)))
            return carry

        lax.fori_loop(0, BLK // 32, adam_rows, 0)

    def add_inner(i):
        for r in (1, 3, 2):
            ucopy(i, r).wait_recv()
        ats = [pl.multiple_of(yy * WIDE + unit_order(z, i) * BLK, BLK) for yy in range(4)]

        def rows_body(k, carry):
            rows = pl.ds(pl.multiple_of(k * 64, 64), 64)
            part = jnp.zeros((64, BLK), F32) if i == 0 else acc[rows, :]
            for yy in range(4):
                x = xv[rows, pl.ds(ats[yy], BLK)].astype(F32)
                part = part + ur[i][yy, rows, :].astype(F32) * x
            acc[rows, :] = part
            return carry

        lax.fori_loop(0, ROWS // 64, rows_body, 0)

    for c in (0, 1):
        add_inner(c)

        @pl.when(z > 0)
        def _():
            sums_in(z, c, rr, RR)

        @pl.when(z < 3)
        def _():
            sums_in(z, c, rl, RL)

        adam(c)

    for copy in sent:
        copy.wait_send()
    for q in range(4):
        for s, right, left in (
            (0, z < 3, z > 0),
            (1, (z == 1) | (z == 2), (z == 1) | (z == 2)),
            (2, z == 2, z == 1),
        ):
            @pl.when(right)
            def _():
                wright(s, q).wait_send()

            @pl.when(left)
            def _():
                wleft(s, q).wait_send()

        for s in (2, 3):
            @pl.when(z == 3)
            def _():
                far(3 - s, q).wait_send()

            @pl.when(z == 0)
            def _():
                far(s, q).wait_send()

    for h in (0, 1):
        for b in range(4):
            @pl.when(z < b)
            def _():
                rsright(b, h).wait_send()

            @pl.when(z > b)
            def _():
                rsleft(b, h).wait_send()

    add_inner(2)
    for copy in sent_units[:9]:
        copy.wait_send()
    add_inner(3)
    for copy in sent_units[9:]:
        copy.wait_send()


def finish_kernel(
    ur0, ur1, ur2, ur3, x, sc, acc, nw, nm, nv, ng, ngm, ngv,
    ig, nw_out, nm_out, nv_out, ng_out, ngm_out, ngv_out,
    grad, sem, grad_sem,
):
    writes = [
        pltpu.make_async_copy(nw, nw_out, sem.at[0]),
        pltpu.make_async_copy(nm, nm_out, sem.at[1]),
        pltpu.make_async_copy(nv, nv_out, sem.at[2]),
    ]
    for c in writes:
        c.start()
    ng_out[...] = ng[...]
    ngm_out[...] = ngm[...]
    ngv_out[...] = ngv[...]

    z = lax.axis_index("fsdp") % 4
    blocks = []
    for i, ref in enumerate((ur0, ur1, ur2, ur3)):
        for yy in range(4):
            at = pl.multiple_of(yy * WIDE + unit_order(z, i) * BLK, BLK)
            blocks.append((ref, yy, pl.ds(at, BLK)))

    def grad_rows(i, carry):
        rows = pl.ds(pl.multiple_of(i * 32, 32), 32)
        s = sc[rows, :]
        t = jnp.sum(acc[rows, :], axis=1, keepdims=True) * (1.0 / 4096)
        t = jnp.broadcast_to(t, (32, 128)) * (s * s * s)
        s, t = (jnp.concatenate([v, v], axis=1) for v in (s, t))
        for ref, yy, cols in blocks:
            grad[rows, cols] = s * ref[yy, rows, :].astype(F32) - x[rows, cols].astype(F32) * t
        return carry

    parts = grad_sem.shape[0]
    size = ROWS // parts
    for p in range(parts):
        lax.fori_loop(p * size // 32, (p + 1) * size // 32, grad_rows, 0)
        rows = pl.ds(p * size, size)
        c = pltpu.make_async_copy(grad.at[rows], ig.at[rows], grad_sem.at[p])
        c.start()
        writes.append(c)
    for c in writes:
        c.wait()


def body(inputs, value_grad, weight, weight_m, weight_v, gain, gain_m, gain_v, mixing):
    vmem = pl.BlockSpec(memory_space=pltpu.VMEM)
    hbm = pl.BlockSpec(memory_space=pl.ANY)
    tokens = inputs.reshape(ROWS, 4 * WIDE)
    shapes = [((ROWS, 4 * WIDE), F32)] + [((BLK, KV), F32)] * 3 + [((1, 1, BLK), F32)] * 3
    passed = [((4, ROWS, BLK), BF16)] * 4 + [((ROWS, 4 * WIDE), BF16), ((ROWS, 128), F32), ((ROWS, BLK), F32)]
    parts = pl.pallas_call(
        step_kernel,
        name="gossip_step",
        out_shape=[pltpu.VMEM(*a) for a in passed + shapes[1:]],
        in_specs=[pl.BlockSpec(memory_space=pltpu.SMEM)] + [hbm] * 5 + [vmem] * 3,
        out_specs=[vmem] * 13,
        scratch_shapes=[
            pltpu.VMEM((BLK, KV), F32),
            pltpu.VMEM((BLK, KV), F32),
            pltpu.VMEM((BLK, KV), F32),
            pltpu.VMEM((4 * ROWS, KV), BF16),
            pltpu.VMEM((4, 4, ROWS, BLK), BF16),
            pltpu.VMEM((4, 4 * ROWS, BLK), BF16),
            pltpu.VMEM((BLK, 4 * ROWS), BF16),
            pltpu.VMEM((4, WROWS, KV), BF16),
            pltpu.VMEM((4, 4 * ROWS, BLK), BF16),
            pltpu.VMEM((4, BLK, KV), F32),
            pltpu.VMEM((4, BLK, KV), BF16),
            pltpu.VMEM((4, BLK, KV), BF16),
            pltpu.VMEM((4, BLK, KV), BF16),
            pltpu.VMEM((4, 8, BLK), F32),
            pltpu.VMEM((3, 8, BLK), F32),
            pltpu.VMEM((4, WROWS, KV), BF16),
            pltpu.VMEM((BLK, 128), F32),
            pltpu.SemaphoreType.DMA((5,)),
            pltpu.SemaphoreType.DMA((NSEM,)),
            pltpu.SemaphoreType.DMA((NSEM,)),
        ],
        compiler_params=pltpu.CompilerParams(
            collective_id=0, has_side_effects=True, vmem_limit_bytes=50 << 20
        ),
    )(
        mixing,
        tokens,
        value_grad.reshape(ROWS, KV),
        weight[0, 0],
        weight_m[0, 0],
        weight_v[0, 0],
        gain,
        gain_m,
        gain_v,
    )
    ig, nw, nm, nv, ng, ngm, ngv = pl.pallas_call(
        finish_kernel,
        name="finish",
        out_shape=[jax.ShapeDtypeStruct(*a) for a in shapes],
        in_specs=[vmem] * 13,
        out_specs=[hbm] * 4 + [vmem] * 3,
        scratch_shapes=[
            pltpu.VMEM((ROWS, 4 * WIDE), F32),
            pltpu.SemaphoreType.DMA((3,)),
            pltpu.SemaphoreType.DMA((4,)),
        ],
        compiler_params=pltpu.CompilerParams(vmem_limit_bytes=16 << 20),
    )(*parts)
    return (ig.reshape(inputs.shape), nw[None, None], nm[None, None], nv[None, None], ng, ngm, ngv)


def solution(mesh):
    placed = (
        P("rx", "ry", None, "fsdp", None),
        P("rx", "ry", None, "fsdp", None),
        P("rx", "ry", "fsdp", None),
        P("rx", "ry", "fsdp", None),
        P("rx", "ry", "fsdp", None),
        P("rx", "ry", "fsdp"),
        P("rx", "ry", "fsdp"),
        P("rx", "ry", "fsdp"),
        P("rx", "ry", None),
    )
    return jax.shard_map(
        body,
        mesh=mesh,
        in_specs=placed,
        out_specs=(
            P("rx", "ry", None, "fsdp", None),
            P("rx", "ry", "fsdp", None),
            P("rx", "ry", "fsdp", None),
            P("rx", "ry", "fsdp", None),
            P("rx", "ry", "fsdp"),
            P("rx", "ry", "fsdp"),
            P("rx", "ry", "fsdp"),
        ),
        check_vma=False,
    )
```

```python
import jax
import jax.numpy as jnp
from jax import lax
from jax.experimental import pallas as pl
from jax.experimental.pallas import tpu as pltpu
from jax.sharding import PartitionSpec as P

MESH = pl.DeviceIdType.MESH
F32 = jnp.float32
BF16 = jnp.bfloat16

ROWS = 256
BLK = 256
KV = 1024
WIDE = 1024
WROWS = BLK + 16

VG = 0
WL = 12
WR = 28
NS = 44
US = 56
RR = 68
RL = 76
GG = 84
GO = 87
NSEM = 94


def KC(k):
    for lo, c in ((87, "GO"), (84, "GG"), (68, "RS"), (56, "US"), (44, "NS"), (12, "W"), (0, "VG")):
        if k >= lo:
            return c


def mirrored(z, codes, i):
    upper = z // 2
    near = z + upper * (3 - 2 * z)
    t = ((codes[0] + (codes[1] - codes[0]) * near) // 4**i) % 4
    return t + upper * (3 - 2 * t)


def grad_order(z, i):
    return mirrored(z, (27, 99), i)


def unit_order(z, i):
    return mirrored(z, (216, 225), i)


def step_kernel(
    mix, x_hbm, vg_hbm, w_hbm, m_hbm, v_hbm, gain, gain_m, gain_v,
    ur0, ur1, ur2, ur3, xv, sc, acc, nw, nm, nv, ng, ngm, ngv,
    wf, mv, vv, vgp, nown, npool, npt, wp, us, gbuf, rsend, rr, rl, gg, ggr, gos, gcol,
    lsem, ssem, rsem,
):
    ur = (ur0, ur1, ur2, ur3)
    rx = lax.axis_index("rx")
    ry = lax.axis_index("ry")
    f = lax.axis_index("fsdp")
    zh = rx // 2
    core = rx % 2
    y = f // 4
    z = f % 4

    def dev(yy, zz):
        return (rx, ry, yy * 4 + zz)

    def ypeer(r):
        return dev((y + r) % 4, z)

    far_rx = (1 - zh) * 2 + (1 - core)
    chip_rx = zh * 2 + (1 - core)

    def remote(src, dst, k, device):
        return pltpu.make_async_remote_copy(
            src_ref=src, dst_ref=dst, send_sem=ssem.at[k], recv_sem=rsem.at[k],
            device_id=device, device_id_type=MESH,
        )

    barrier = pltpu.get_barrier_semaphore()
    far_base = (1 - z // 2) * 2
    partners = [ypeer(1), ypeer(2), ypeer(3)]
    partners += [dev(y, (z + 1) % 4), dev(y, (z + 2) % 4), dev(y, (z + 3) % 4)]
    partners += [(rx, (ry + 1) % 4, f), (rx, (ry + 3) % 4, f), (chip_rx, ry, f)]
    partners += [(far_rx, ry, y * 4 + far_base), (far_rx, ry, y * 4 + far_base + 1)]
    for p in partners:
        pl.semaphore_signal(barrier, inc=1, device_id=p, device_id_type=MESH)
    loads = [
        pltpu.make_async_copy(w_hbm, wf, lsem.at[0]),
        pltpu.make_async_copy(x_hbm, xv, lsem.at[1]),
        pltpu.make_async_copy(vg_hbm, vgp.at[pl.ds(0, ROWS)], lsem.at[2]),
        pltpu.make_async_copy(m_hbm, mv, lsem.at[3]),
        pltpu.make_async_copy(v_hbm, vv, lsem.at[4]),
    ]
    for k in (0, 1):
        loads[k].start()

    pl.semaphore_wait(barrier, len(partners))

    sent, sent_units = [], []

    def go(copy, to=sent):
        copy.start()
        to.append(copy)

    def half(ref, slot, h, c):
        return ref.at[pl.ds(slot * ROWS + h * (ROWS // 2), ROWS // 2), pl.ds(c * (KV // 2), KV // 2)]

    def vg_own(c):
        for k, (r, h) in enumerate(((1, 0), (3, 1), (1, 1), (3, 0))):
            go(remote(half(vg_hbm, 0, h, c), half(vgp, r, h, c), VG + 6 * c + k, ypeer(r)))

    def vg_arrived(c, k, slot, h):
        remote(half(vgp, slot, h, c), half(vgp, slot, h, c), VG + 6 * c + k, ypeer(1)).wait_recv()

    def vg_relay(c):
        for k, (r, h) in enumerate(((1, 0), (3, 1))):
            vg_arrived(c, k, r, h)
            go(remote(half(vgp, r, h, c), half(vgp, 2, h, c), VG + 6 * c + 4 + k, ypeer(r)))

    def vg_all(c):
        for k, (r, h) in ((2, (1, 1)), (3, (3, 0)), (4, (2, 0)), (5, (2, 1))):
            vg_arrived(c, k, r, h)

    vg_own(0)
    for k in (2, 3, 4):
        loads[k].start()

    loads[0].wait()
    gain_row = gain[0].astype(BF16)

    def cast_rows(i, carry):
        rows = pl.ds(pl.multiple_of(i * 32, 32), 32)
        wp[z, rows, :] = wf[rows, :].astype(BF16)
        return carry

    lax.fori_loop(0, BLK // 32, cast_rows, 0)
    wp[z, BLK:WROWS, :] = jnp.zeros((16, KV), BF16)
    wp[z, BLK:WROWS, 0:BLK] = jnp.broadcast_to(gain_row.astype(F32), (16, BLK)).astype(BF16)


    def quarter(ref, block, q):
        return ref.at[block, pl.ds(q * 64, 64 + 16 * (q // 3))]

    def wright(s, q):
        return remote(quarter(wp, z - s, q), quarter(wp, z - s, q), WL + 4 * s + q, dev(y, z + 1))

    def wleft(s, q):
        return remote(quarter(wp, z + s, q), quarter(wp, z + s, q), WR + 4 * s + q, dev(y, z - 1))

    def from_left(s, q):
        remote(quarter(wp, z - s, q), quarter(wp, z - s, q), WL + 4 * s + q - 4, dev(y, z)).wait_recv()

    def from_right(s, q):
        remote(quarter(wp, z + s, q), quarter(wp, z + s, q), WR + 4 * s + q - 4, dev(y, z)).wait_recv()

    def far(zz, q):
        return remote(quarter(wp, zz, q), quarter(gos, 3, q), GO + 3 + q, (far_rx, ry, y * 4 + zz))

    @pl.when(z < 3)
    def _():
        wright(0, 0).start()

    @pl.when(z > 0)
    def _():
        wleft(0, 0).start()

    @pl.when(z < 2)
    def _():
        for q in (1, 2, 3):
            wright(0, q).start()

    @pl.when(z > 1)
    def _():
        for q in (1, 2, 3):
            wleft(0, q).start()

    go(remote(wp.at[z], gos.at[2], GO + 2, (chip_rx, ry, f)))
    go(remote(wp.at[z], gos.at[0], GO + 0, (rx, (ry + 1) % 4, f)))
    go(remote(wp.at[z], gos.at[1], GO + 1, (rx, (ry + 3) % 4, f)))

    vg_relay(0)

    loads[1].wait()

    def norm_rows(i, carry):
        rows = pl.ds(pl.multiple_of(i * 64, 64), 64)
        part = jnp.zeros((64, 128), F32)
        for c in range(4 * WIDE // 128):
            x = xv[rows, c * 128:(c + 1) * 128].astype(F32)
            part = part + x * x
        s = lax.rsqrt(jnp.sum(part, axis=1, keepdims=True) * (1.0 / 4096) + 1e-05)
        s = jnp.broadcast_to(s, (64, 128))
        sc[rows, :] = s
        for yy in range(4):
            for b in range(4):
                for c in (0, 128):
                    at = yy * WIDE + b * BLK + c
                    nown[yy, b, rows, c:c + 128] = (xv[rows, at:at + 128].astype(F32) * s).astype(BF16)
        return carry

    lax.fori_loop(0, ROWS // 64, norm_rows, 0)

    def outwards(q):
        @pl.when(z == 2)
        def _():
            from_left(1, q)
            wright(1, q).start()

        @pl.when(z == 1)
        def _():
            from_right(1, q)
            wleft(1, q).start()

    outwards(0)

    def order(i):
        return grad_order(z, i)

    def slot(r):
        return pl.ds(r * ROWS, ROWS)

    def ncopy(i, r):
        b = order(i)
        return remote(nown.at[(y + r) % 4, b], npool.at[b, slot(r)], NS + 3 * i + r - 1, ypeer(r))

    for r in (1, 3, 2):
        go(ncopy(0, r))
    vg_own(1)

    def own_rows(i, carry):
        rows = pl.ds(pl.multiple_of(i * 64, 64), 64)
        for b in range(4):
            npool[b, rows, :] = nown[y, b, rows, :]
        return carry

    lax.fori_loop(0, ROWS // 64, own_rows, 0)

    def part(ref, b, c):
        return ref.at[b, :, pl.ds(c * (KV // 2), KV // 2)]

    def rsright(b, c):
        return remote(part(rsend, b, c), part(rr, b, c), RR + 2 * b + c, dev(y, z + 1))

    def rsleft(b, c):
        return remote(part(rsend, b, c), part(rl, b, c), RL + 2 * b + c, dev(y, z - 1))

    def sums_in(b, c, ref, k):
        remote(part(rsend, b, c), part(ref, b, c), k + 2 * b + c, dev(y, z)).wait_recv()

    def round_half(b, c, other=None):
        cols = pl.ds(c * (KV // 2), KV // 2)

        def rows_body(i, carry):
            rows = pl.ds(pl.multiple_of(i * 32, 32), 32)
            g = gbuf[b, rows, cols]
            if other is not None:
                g = g + other[b, rows, cols].astype(F32)
            rsend[b, rows, cols] = g.astype(BF16)
            return carry

        lax.fori_loop(0, BLK // 32, rows_body, 0)

    def weight_grad(i, c):
        b = order(i)
        if c == 0:
            for r in (1, 3, 2):
                ncopy(i, r).wait_recv()
            npt[...] = npool[b].T

        def columns(k, carry):
            cols = pl.ds(pl.multiple_of(c * (KV // 2) + k * 256, 256), 256)
            gbuf[b, :, cols] = jnp.dot(npt[...], vgp[:, cols], preferred_element_type=F32)
            return carry

        lax.fori_loop(0, KV // 512, columns, 0)
        if i < 3:
            @pl.when(z == 0)
            def _():
                round_half(3 - i, c)
                rsright(3 - i, c).start()

            @pl.when(z == 3)
            def _():
                round_half(i, c)
                rsleft(i, c).start()

    def ucopy(i, r):
        b = unit_order(z, i)
        return remote(us.at[b, slot(r)], ur[i].at[y], US + 3 * i + r - 1, ypeer(4 - r))

    def unit_grad(i):
        b = unit_order(z, i)
        gl = wp[b, BLK:WROWS, 0:BLK].astype(F32)[0:1, :]

        def tokens(r, carry):
            rows = pl.ds(pl.multiple_of(r * ROWS, ROWS), ROWS)
            og = lax.dot_general(
                vgp[rows, :], wp[b, 0:BLK, :], (((1,), (1,)), ((), ())), preferred_element_type=F32
            )
            us[b, rows, :] = (og * gl).astype(BF16)
            return carry

        lax.fori_loop(0, 4, tokens, 0)
        for r in (2, 1, 3):
            go(ucopy(i, r), sent_units)
        ur[i][y] = us[b, 0:ROWS, :]

    eye = lax.broadcasted_iota(jnp.int32, (BLK, BLK), 0) == lax.broadcasted_iota(jnp.int32, (BLK, BLK), 1)

    def gain_grad(b):
        def rows_body(i, carry):
            rows = pl.ds(pl.multiple_of(i * 64, 64), 64)
            part = jnp.zeros((64, 128), F32)
            for c in range(KV // 128):
                cols = pl.ds(c * 128, 128)
                part = part + wp[b, rows, cols].astype(F32) * gbuf[b, rows, cols]
            gcol[rows, :] = part
            return carry

        lax.fori_loop(0, BLK // 64, rows_body, 0)
        col = jnp.sum(gcol[...], axis=1, keepdims=True)
        spread = jnp.where(eye, jnp.broadcast_to(col, (BLK, BLK)), 0.0)
        gg[b] = jnp.sum(spread.reshape(BLK // 8, 8, BLK), axis=0)

    def relay_right(s):
        for q in range(4):
            from_left(s, q)
            wright(s, q).start()

    def relay_left(s):
        for q in range(4):
            from_right(s, q)
            wleft(s, q).start()

    def gossip_out(s, q):
        @pl.when(z == 3)
        def _():
            from_left(s, q)
            far(3 - s, q).start()

        @pl.when(z == 0)
        def _():
            from_right(s, q)
            far(s, q).start()

    def forward_right(b, c):
        sums_in(b, c, rr, RR)
        round_half(b, c, rr)
        rsright(b, c).start()

    def forward_left(b, c):
        sums_in(b, c, rl, RL)
        round_half(b, c, rl)
        rsleft(b, c).start()

    def forward_first(h):
        @pl.when(z == 1)
        def _():
            forward_right(3, h)

        @pl.when(z == 2)
        def _():
            forward_left(0, h)

    def forward_second(h):
        @pl.when(z == 1)
        def _():
            forward_left(0, h)
            forward_right(2, h)

        @pl.when(z == 2)
        def _():
            forward_right(3, h)
            forward_left(1, h)

    outwards(1)
    gossip_out(2, 0)
    outwards(2)
    gossip_out(2, 1)
    outwards(3)
    gossip_out(2, 2)
    vg_relay(1)
    for i in (1, 2, 3):
        for r in (1, 3, 2):
            go(ncopy(i, r))

    @pl.when(z == 2)
    def _():
        for q in (1, 2, 3):
            wright(0, q).start()
        relay_left(1)

    @pl.when(z == 1)
    def _():
        for q in (1, 2, 3):
            wleft(0, q).start()
        relay_right(1)

    loads[2].wait()
    gossip_out(2, 3)
    vg_all(0)
    weight_grad(0, 0)
    vg_all(1)
    weight_grad(0, 1)
    unit_grad(0)

    @pl.when(z == 2)
    def _():
        relay_right(2)

    @pl.when(z == 1)
    def _():
        relay_left(2)

    unit_grad(1)
    weight_grad(1, 0)
    weight_grad(1, 1)
    forward_first(0)

    @pl.when(z == 3)
    def _():
        for q in range(4):
            from_left(1, q)

    @pl.when(z == 0)
    def _():
        for q in range(4):
            from_right(1, q)

    unit_grad(2)
    weight_grad(2, 0)
    weight_grad(2, 1)
    for q in range(4):
        gossip_out(3, q)
    forward_first(1)
    unit_grad(3)
    weight_grad(3, 0)
    weight_grad(3, 1)
    forward_second(0)

    def gain_block(b, carry):
        gain_grad(b)
        return carry

    lax.fori_loop(0, 4, gain_block, 0)

    def ggcopy(d):
        zz = (z + d) % 4
        return remote(gg.at[zz], ggr.at[d - 1], GG + d - 1, dev(y, zz))

    for d in (1, 2, 3):
        go(ggcopy(d))

    forward_second(1)

    total = (mix[0, 0, 0] + mix[0, 0, 1] + mix[0, 0, 2] + mix[0, 0, 3] + mix[0, 0, 4]).astype(F32)

    def share(n, width):
        return jnp.full((1, width), mix[0, 0, n].astype(F32), F32) / jnp.full((1, width), total, F32)

    from_chip, from_far = 2 - core, 1 + core

    for d in (1, 2, 3):
        ggcopy(d).wait_recv()
    g8 = gg[z] + ggr[0] + ggr[1] + ggr[2]
    grad_gain = jnp.sum(g8, axis=0, keepdims=True)
    own_gain = gain[0]
    new_gm = 0.9 * gain_m[0] + 0.1 * grad_gain
    new_gv = 0.999 * gain_v[0] + 0.001 * grad_gain * grad_gain
    ngm[0] = new_gm
    ngv[0] = new_gv
    stepped_g = own_gain - 0.01 * new_gm / (jnp.sqrt(new_gv) + 1e-08)

    remote(gos.at[2], gos.at[2], GO + 2, dev(y, z)).wait_recv()
    remote(gos.at[0], gos.at[0], GO + 0, dev(y, z)).wait_recv()
    remote(gos.at[1], gos.at[1], GO + 1, dev(y, z)).wait_recv()
    for q in range(4):
        far_in = quarter(gos, 3, q)
        remote(far_in, far_in, GO + 3 + q, dev(y, z)).wait_recv()

    def gossip_gain(n):
        return gos[n, BLK:WROWS, 0:BLK].astype(F32)[0:1, :]

    mixed_g = share(0, BLK) * stepped_g
    mixed_g = mixed_g + share(3, BLK) * gossip_gain(0) + share(4, BLK) * gossip_gain(1)
    mixed_g = mixed_g + share(from_chip, BLK) * gossip_gain(2) + share(from_far, BLK) * gossip_gain(3)
    ng[0] = mixed_g

    col = jnp.sum(jnp.where(eye, jnp.broadcast_to(gain_row.astype(F32), (BLK, BLK)), 0.0), axis=1, keepdims=True)
    gcol[...] = jnp.broadcast_to(col, (BLK, 128))

    @pl.when(z == 0)
    def _():
        rr[z] = jnp.zeros((BLK, KV), BF16)

    @pl.when(z == 3)
    def _():
        rl[z] = jnp.zeros((BLK, KV), BF16)

    loads[3].wait()
    loads[4].wait()
    s0, s1, s2 = share(0, KV // 2), share(3, KV // 2), share(4, KV // 2)
    s3, s4 = share(from_chip, KV // 2), share(from_far, KV // 2)

    for c in (0, 1):
        cols = pl.ds(c * (KV // 2), KV // 2)

        def mix_rows(i, carry):
            rows = pl.ds(pl.multiple_of(i * 32, 32), 32)
            own = wf[rows, cols]
            out = s0 * (own - 0.01 * (0.1 * own))
            out = out + s1 * gos[0, rows, cols].astype(F32) + s2 * gos[1, rows, cols].astype(F32)
            nw[rows, cols] = out + s3 * gos[2, rows, cols].astype(F32) + s4 * gos[3, rows, cols].astype(F32)
            return carry

        lax.fori_loop(0, BLK // 32, mix_rows, 0)

    def adam(c):
        cols = pl.ds(c * (KV // 2), KV // 2)

        def adam_rows(i, carry):
            rows = pl.ds(pl.multiple_of(i * 32, 32), 32)
            g = gbuf[z, rows, cols] + rr[z, rows, cols].astype(F32) + rl[z, rows, cols].astype(F32)
            g = gcol[rows, 0:1] * g
            new_m = 0.9 * mv[rows, cols] + 0.1 * g
            new_v = 0.999 * vv[rows, cols] + 0.001 * g * g
            nm[rows, cols] = new_m
            nv[rows, cols] = new_v
            nw[rows, cols] = nw[rows, cols] - s0 * (0.01 * (new_m / (jnp.sqrt(new_v) + 1e-08)))
            return carry

        lax.fori_loop(0, BLK // 32, adam_rows, 0)

    def add_inner(i):
        for r in (1, 3, 2):
            ucopy(i, r).wait_recv()
        ats = [pl.multiple_of(yy * WIDE + unit_order(z, i) * BLK, BLK) for yy in range(4)]

        def rows_body(k, carry):
            rows = pl.ds(pl.multiple_of(k * 64, 64), 64)
            part = jnp.zeros((64, BLK), F32) if i == 0 else acc[rows, :]
            for yy in range(4):
                x = xv[rows, pl.ds(ats[yy], BLK)].astype(F32)
                part = part + ur[i][yy, rows, :].astype(F32) * x
            acc[rows, :] = part
            return carry

        lax.fori_loop(0, ROWS // 64, rows_body, 0)

    for c in (0, 1):
        add_inner(c)

        @pl.when(z > 0)
        def _():
            sums_in(z, c, rr, RR)

        @pl.when(z < 3)
        def _():
            sums_in(z, c, rl, RL)

        adam(c)

    for copy in sent:
        copy.wait_send()
    for q in range(4):
        for s, right, left in (
            (0, z < 3, z > 0),
            (1, (z == 1) | (z == 2), (z == 1) | (z == 2)),
            (2, z == 2, z == 1),
        ):
            @pl.when(right)
            def _():
                wright(s, q).wait_send()

            @pl.when(left)
            def _():
                wleft(s, q).wait_send()

        for s in (2, 3):
            @pl.when(z == 3)
            def _():
                far(3 - s, q).wait_send()

            @pl.when(z == 0)
            def _():
                far(s, q).wait_send()

    for h in (0, 1):
        for b in range(4):
            @pl.when(z < b)
            def _():
                rsright(b, h).wait_send()

            @pl.when(z > b)
            def _():
                rsleft(b, h).wait_send()

    add_inner(2)
    for copy in sent_units[:9]:
        copy.wait_send()
    add_inner(3)
    for copy in sent_units[9:]:
        copy.wait_send()


def finish_kernel(
    ur0, ur1, ur2, ur3, x, sc, acc, nw, nm, nv, ng, ngm, ngv,
    ig, nw_out, nm_out, nv_out, ng_out, ngm_out, ngv_out,
    grad, sem, grad_sem,
):
    writes = [
        pltpu.make_async_copy(nw, nw_out, sem.at[0]),
        pltpu.make_async_copy(nm, nm_out, sem.at[1]),
        pltpu.make_async_copy(nv, nv_out, sem.at[2]),
    ]
    for c in writes:
        c.start()
    ng_out[...] = ng[...]
    ngm_out[...] = ngm[...]
    ngv_out[...] = ngv[...]

    z = lax.axis_index("fsdp") % 4
    blocks = []
    for i, ref in enumerate((ur0, ur1, ur2, ur3)):
        for yy in range(4):
            at = pl.multiple_of(yy * WIDE + unit_order(z, i) * BLK, BLK)
            blocks.append((ref, yy, pl.ds(at, BLK)))

    def grad_rows(i, carry):
        rows = pl.ds(pl.multiple_of(i * 32, 32), 32)
        s = sc[rows, :]
        t = jnp.sum(acc[rows, :], axis=1, keepdims=True) * (1.0 / 4096)
        t = jnp.broadcast_to(t, (32, 128)) * (s * s * s)
        s, t = (jnp.concatenate([v, v], axis=1) for v in (s, t))
        for ref, yy, cols in blocks:
            grad[rows, cols] = s * ref[yy, rows, :].astype(F32) - x[rows, cols].astype(F32) * t
        return carry

    parts = grad_sem.shape[0]
    size = ROWS // parts
    for p in range(parts):
        lax.fori_loop(p * size // 32, (p + 1) * size // 32, grad_rows, 0)
        rows = pl.ds(p * size, size)
        c = pltpu.make_async_copy(grad.at[rows], ig.at[rows], grad_sem.at[p])
        c.start()
        writes.append(c)
    for c in writes:
        c.wait()


def body(inputs, value_grad, weight, weight_m, weight_v, gain, gain_m, gain_v, mixing):
    vmem = pl.BlockSpec(memory_space=pltpu.VMEM)
    hbm = pl.BlockSpec(memory_space=pl.ANY)
    tokens = inputs.reshape(ROWS, 4 * WIDE)
    shapes = [((ROWS, 4 * WIDE), F32)] + [((BLK, KV), F32)] * 3 + [((1, 1, BLK), F32)] * 3
    passed = [((4, ROWS, BLK), BF16)] * 4 + [((ROWS, 4 * WIDE), BF16), ((ROWS, 128), F32), ((ROWS, BLK), F32)]
    parts = pl.pallas_call(
        step_kernel,
        name="gossip_step",
        out_shape=[pltpu.VMEM(*a) for a in passed + shapes[1:]],
        in_specs=[pl.BlockSpec(memory_space=pltpu.SMEM)] + [hbm] * 5 + [vmem] * 3,
        out_specs=[vmem] * 13,
        scratch_shapes=[
            pltpu.VMEM((BLK, KV), F32),
            pltpu.VMEM((BLK, KV), F32),
            pltpu.VMEM((BLK, KV), F32),
            pltpu.VMEM((4 * ROWS, KV), BF16),
            pltpu.VMEM((4, 4, ROWS, BLK), BF16),
            pltpu.VMEM((4, 4 * ROWS, BLK), BF16),
            pltpu.VMEM((BLK, 4 * ROWS), BF16),
            pltpu.VMEM((4, WROWS, KV), BF16),
            pltpu.VMEM((4, 4 * ROWS, BLK), BF16),
            pltpu.VMEM((4, BLK, KV), F32),
            pltpu.VMEM((4, BLK, KV), BF16),
            pltpu.VMEM((4, BLK, KV), BF16),
            pltpu.VMEM((4, BLK, KV), BF16),
            pltpu.VMEM((4, 8, BLK), F32),
            pltpu.VMEM((3, 8, BLK), F32),
            pltpu.VMEM((4, WROWS, KV), BF16),
            pltpu.VMEM((BLK, 128), F32),
            pltpu.SemaphoreType.DMA((5,)),
            pltpu.SemaphoreType.DMA((NSEM,)),
            pltpu.SemaphoreType.DMA((NSEM,)),
        ],
        compiler_params=pltpu.CompilerParams(
            collective_id=0, has_side_effects=True, vmem_limit_bytes=50 << 20
        ),
    )(
        mixing,
        tokens,
        value_grad.reshape(ROWS, KV),
        weight[0, 0],
        weight_m[0, 0],
        weight_v[0, 0],
        gain,
        gain_m,
        gain_v,
    )
    ig, nw, nm, nv, ng, ngm, ngv = pl.pallas_call(
        finish_kernel,
        name="finish",
        out_shape=[jax.ShapeDtypeStruct(*a) for a in shapes],
        in_specs=[vmem] * 13,
        out_specs=[hbm] * 4 + [vmem] * 3,
        scratch_shapes=[
            pltpu.VMEM((ROWS, 4 * WIDE), F32),
            pltpu.SemaphoreType.DMA((3,)),
            pltpu.SemaphoreType.DMA((4,)),
        ],
        compiler_params=pltpu.CompilerParams(vmem_limit_bytes=16 << 20),
    )(*parts)
    return (ig.reshape(inputs.shape), nw[None, None], nm[None, None], nv[None, None], ng, ngm, ngv)


def solution(mesh):
    placed = (
        P("rx", "ry", None, "fsdp", None),
        P("rx", "ry", None, "fsdp", None),
        P("rx", "ry", "fsdp", None),
        P("rx", "ry", "fsdp", None),
        P("rx", "ry", "fsdp", None),
        P("rx", "ry", "fsdp"),
        P("rx", "ry", "fsdp"),
        P("rx", "ry", "fsdp"),
        P("rx", "ry", None),
    )
    return jax.shard_map(
        body,
        mesh=mesh,
        in_specs=placed,
        out_specs=(
            P("rx", "ry", None, "fsdp", None),
            P("rx", "ry", "fsdp", None),
            P("rx", "ry", "fsdp", None),
            P("rx", "ry", "fsdp", None),
            P("rx", "ry", "fsdp"),
            P("rx", "ry", "fsdp"),
            P("rx", "ry", "fsdp"),
        ),
        check_vma=False,
    )
```
